32 devices in a mesh: dom: 16 (over z, y, x), col: 2 (over core).
Axes of the slice: x: 2, y: 2, z: 4, core: 2. Of those that a mesh axis runs over, the one named last changes fastest.
Arguments:
- adjoint_rhs: bfloat16 [3072, 105, 64], P('dom', None, 'col')
- element_blocks: bfloat16 [1536, 420, 420], P('dom', 'col')
- element_faces: int32 [1536, 4], P('dom'), may hold values from 0 to 239, as said below
- send_faces: int32 [16, 48], P('dom'), may hold values from 0 to 191
Outputs:
- second_basis: bfloat16 [3072, 105, 64], P('dom', None, 'col')
- next_vector: bfloat16 [3072, 105, 64], P('dom', None, 'col')
- hessenberg: float32 [5, 64], P(None, 'col')
The draws below stay inside these ranges and needn't reach their ends.
Inputs may be any that keep to these rules, and one draw needn't show every extreme that they name: `element_faces`: row d * 96 + e belongs to partition d. An entry below 192 is an owned face; an entry 192 + p * 3 + s stands for the face that partition p lists in send_faces at position d * 3 + s. No partition names one of its slots at or above 192 twice, and none names its own index p = d.
All inputs are finite; a program needn't handle non-finite values.
Results may differ from the reference program's by a relative error of at most 0.02.
Values may be sent and summed in bfloat16 or wider, within the bound.
No kernel may reach another device: no remote copies, remote signals or barrier semaphores. Data moves between devices by JAX's collectives and lax.ppermute only.
A program may use at most 192 MiB of HBM per device.

```python
import math
import jax
import jax.numpy as jnp
from jax import lax

P_SIZE = 105
E_DEV = 96
F_DEV = 192
SLOT = 3
NRHS = 64
FACES = 3072
N_DOM = 16
N_COL = 2


def draw_adjoint_rhs(key, part):
    key_normal, key_rows, key_cols = jax.random.split(key, 3)
    position = jnp.arange(FACES, dtype=jnp.float32) / FACES
    row_scale = 3.0 ** position * 10.0 ** jax.random.uniform(key_rows, (FACES,), jnp.float32)
    col_scale = 10.0 ** jax.random.uniform(key_cols, (NRHS,), jnp.float32)
    normal_part = jax.random.normal(key_normal, (FACES, P_SIZE, NRHS), jnp.float32)
    return (0.3 * normal_part * row_scale[:, None, None] * col_scale[None, None, :]).astype(jnp.bfloat16)


def draw_element_blocks(key, part):
    key_noise, key_diag = jax.random.split(key)
    row_count = N_DOM * E_DEV
    block_width = 4 * P_SIZE
    noise_part = jax.random.normal(key_noise, (row_count, block_width, block_width), jnp.float32)
    diagonal = jnp.exp(jax.random.uniform(key_diag, (row_count, block_width), jnp.float32, minval=math.log(0.5), maxval=math.log(2.0)))
    identity = jnp.eye(block_width, dtype=jnp.float32)
    return (0.8 * noise_part / math.sqrt(block_width) + diagonal[:, :, None] * identity[None]).astype(jnp.bfloat16)


def draw_element_faces(key, part):
    ghosts = SLOT * N_DOM
    key_counts, key_order = jax.random.split(jax.random.fold_in(key, 17))
    counts = jax.random.randint(key_counts, (N_DOM, N_DOM), 0, SLOT + 1)
    sender = jnp.arange(N_DOM)[:, None]
    receiver = jnp.arange(N_DOM)[None, :]
    offset = (sender - receiver) % N_DOM
    forced = (offset == 1) | (offset == N_DOM - 1) | (offset == N_DOM // 2)
    counts = jnp.where(forced, SLOT, counts)
    counts = jnp.where(offset == 0, 0, counts)
    slot_index = jnp.arange(ghosts)
    in_use = slot_index[None, :] % SLOT < counts.T[:, slot_index // SLOT]
    orders = jax.vmap(lambda one_key: jax.random.permutation(one_key, 4 * E_DEV))(jax.random.split(key_order, N_DOM))
    owned_pick = jnp.where(orders < ghosts, orders, orders - ghosts) % F_DEV
    used_pick = jnp.take_along_axis(in_use, jnp.minimum(orders, ghosts - 1), axis=1) & (orders < ghosts)
    face_ids = jnp.where(used_pick, F_DEV + orders, owned_pick)
    return face_ids.reshape(N_DOM * E_DEV, 4).astype(jnp.int32)


def with_ends(values, stream_key, smallest, top_value):
    longest = values.shape.index(max(values.shape))
    spots = []
    for shift in (0, 1):
        where = [jax.random.randint(jax.random.fold_in(stream_key, axis), (), 0, length) for axis, length in enumerate(values.shape)]
        where[longest] = (where[longest] + shift) % values.shape[longest]
        spots.append(tuple(where))
    return values.at[spots[0]].set(smallest).at[spots[1]].set(top_value)


def setup_inputs(seed: int = 0) -> dict:
    keys = jax.random.split(jax.random.key(seed), 5)
    return {
        "adjoint_rhs": draw_adjoint_rhs(jax.random.fold_in(keys[4], 71), 0),
        "element_blocks": draw_element_blocks(jax.random.fold_in(keys[4], 71), 0),
        "element_faces": draw_element_faces(jax.random.fold_in(keys[4], 71), 0),
        "send_faces": with_ends(jax.random.randint(keys[3], (N_DOM, SLOT * N_DOM), 0, F_DEV), jax.random.fold_in(keys[3], 1), 0, F_DEV - 1).astype(jnp.int32),
    }


epsilon = 1e-06

def transposed(vector, element_blocks, element_faces, send_faces):
    owned_count = F_DEV
    ghosts = SLOT * N_DOM
    by_device = vector.reshape(N_DOM, owned_count, P_SIZE, NRHS)
    outgoing = jax.vmap(lambda values, chosen: values[chosen])(by_device, send_faces)
    incoming = outgoing.reshape(N_DOM, N_DOM, SLOT, P_SIZE, NRHS).transpose(1, 0, 2, 3, 4).reshape(N_DOM, ghosts, P_SIZE, NRHS)
    known_traces = jnp.concatenate([by_device, incoming], axis=1)
    matrices = element_blocks.reshape(N_DOM, E_DEV, 4 * P_SIZE, 4 * P_SIZE)
    face_table = element_faces.reshape(N_DOM, E_DEV, 4)
    slot_share = 4 // N_COL

    def device_terms(operands):
        values, blocks_here, faces_here = operands
        picked = values[faces_here].reshape(E_DEV, 4 * P_SIZE, NRHS)
        totals = jnp.zeros((owned_count + ghosts, P_SIZE, NRHS), jnp.float32)
        for column in range(N_COL):
            first_row = column * slot_share * P_SIZE
            last_row = first_row + slot_share * P_SIZE
            partial_terms = jnp.einsum('ekb,ekr->ebr', blocks_here[:, first_row:last_row].astype(jnp.float32), picked[:, first_row:last_row].astype(jnp.float32))
            summed = jax.ops.segment_sum(partial_terms.reshape(E_DEV * 4, P_SIZE, NRHS), faces_here.reshape(-1), num_segments=owned_count + ghosts)
            totals = totals + lax.optimization_barrier(summed.astype(jnp.bfloat16)).astype(jnp.float32)
        return totals
    totals = lax.map(device_terms, (known_traces, matrices, face_table))
    returned = totals[:, owned_count:].reshape(N_DOM, N_DOM, SLOT, P_SIZE, NRHS).transpose(1, 0, 2, 3, 4).reshape(N_DOM, ghosts, P_SIZE, NRHS)
    added = jax.vmap(lambda pieces, chosen: jax.ops.segment_sum(pieces, chosen, num_segments=owned_count))(returned, send_faces)
    return (totals[:, :owned_count] + added).reshape(N_DOM * owned_count, P_SIZE, NRHS)

def reference(adjoint_rhs, element_blocks, element_faces, send_faces):
    entries = FACES * P_SIZE
    residual = adjoint_rhs.astype(jnp.float32)
    start_norm = jnp.sqrt(lax.optimization_barrier(jnp.sum(residual * residual, axis=(0, 1))) / entries + epsilon)
    first_basis = (residual / start_norm).astype(jnp.bfloat16)
    first_image = transposed(first_basis, element_blocks, element_faces, send_faces)
    first_float = first_basis.astype(jnp.float32)
    diagonal_term = lax.optimization_barrier(jnp.sum(first_float * first_image, axis=(0, 1))) / entries
    projected = first_image - diagonal_term * first_float
    next_norm = jnp.sqrt(lax.optimization_barrier(jnp.sum(projected * projected, axis=(0, 1))) / entries + epsilon)
    second_basis = (projected / next_norm).astype(jnp.bfloat16)
    second_image = transposed(second_basis, element_blocks, element_faces, send_faces)
    second_float = second_basis.astype(jnp.float32)
    proj_first = lax.optimization_barrier(jnp.sum(first_float * second_image, axis=(0, 1))) / entries
    proj_second = lax.optimization_barrier(jnp.sum(second_float * second_image, axis=(0, 1))) / entries
    next_vector = (second_image - proj_first * first_float - proj_second * second_float).astype(jnp.bfloat16)
    hessenberg = jnp.stack([start_norm, diagonal_term, next_norm, proj_first, proj_second])
    return (second_basis, next_vector, hessenberg)
```

```python
import functools

import jax
import jax.numpy as jnp
from jax import lax
from jax.experimental import pallas as pl
from jax.experimental.pallas import tpu as pltpu
from jax.sharding import PartitionSpec as P

P_SIZE = 105
LANES = 128
MIB = 1 << 20
TOGETHER = 4

epsilon = 1e-06

f32 = jnp.float32
bf16 = jnp.bfloat16

VMEM = pl.BlockSpec(memory_space=pltpu.VMEM)
SMEM = pl.BlockSpec(memory_space=pltpu.SMEM)
ANY = pl.BlockSpec(memory_space=pl.ANY)


def lane_ids(rows):
    return lax.broadcasted_iota(jnp.int32, (rows, LANES), 1)


def stat_lanes(columns):
    rows = columns[0].shape[0]
    lanes = lane_ids(rows)
    block = jnp.zeros((rows, LANES), f32)
    lane = P_SIZE
    for value in columns:
        rest = value * 0.5
        for _ in range(3):
            part = rest.astype(bf16).astype(f32)
            block = jnp.where(lanes == lane, part, block)
            rest = rest - part
            lane += 1
    return block


def read_stat(block, which):
    lanes = lane_ids(block.shape[0])
    first = P_SIZE + 3 * which
    inside = (lanes >= first) & (lanes < first + 3)
    return 2.0 * jnp.sum(jnp.where(inside, block, 0.0), axis=1, keepdims=True)


def gathered_block(ghost_ref, ranks):
    slots = ghost_ref.shape[0] // ranks
    total = ghost_ref[0].astype(f32)
    for rank in range(1, ranks):
        total = total + ghost_ref[rank * slots].astype(f32)
    return total


def first_payload_kernel(rhs_ref, send_ref, payload_ref):
    faces, rows, _ = rhs_ref.shape

    def add(step, total):
        chunk = rhs_ref[pl.ds(step * 8, 8)].astype(f32)
        return total + jnp.sum(chunk * chunk, axis=0)

    total = lax.fori_loop(0, faces // 8, add, jnp.zeros((rows, P_SIZE), f32))
    stats = stat_lanes([jnp.sum(total, axis=1, keepdims=True)]).astype(bf16)

    @pl.loop(0, payload_ref.shape[0])
    def _(slot):
        payload_ref[slot] = stats
        payload_ref[slot, :, :P_SIZE] = rhs_ref[send_ref[0, slot]]


def relayout_kernel(raw_ref, perm_ref, tail_ref, out_ref, buffer, sems):
    group = buffer.shape[2]
    steps = raw_ref.shape[1] // group
    width = out_ref.shape[2]
    contracted = raw_ref.shape[0]
    slots = contracted // P_SIZE
    full = P_SIZE // group
    rest = P_SIZE - full * group

    def copy(step):
        return pltpu.make_async_copy(
            raw_ref.at[:, pl.ds(pl.multiple_of(step * group, group), group), :], buffer.at[step % 2], sems.at[step % 2]
        )

    copy(0).start()

    @pl.loop(0, steps)
    def _(step):
        @pl.when(step + 1 < steps)
        def _():
            copy(step + 1).start()

        copy(step).wait()
        held = buffer.at[step % 2]
        for slot in range(slots):
            for part in range(full + 1):
                first = slot * P_SIZE + part * group
                depth = group if part < full else rest
                chunk = held[first : first + depth].reshape(depth * group, raw_ref.shape[2])
                perm = perm_ref[...] if part < full else tail_ref[...]
                moved = jnp.dot(perm, chunk, preferred_element_type=f32).astype(bf16)
                for element in range(group):
                    out_ref[
                        step * group + element, pl.ds(slot * LANES + part * group, group), : raw_ref.shape[2]
                    ] = moved[element * group : (element + 1) * group]
        zeros = jnp.zeros((LANES - (full + 1) * group, width), bf16)
        for element in range(group):
            for slot in range(slots):
                out_ref[step * group + element, pl.ds(slot * LANES + (full + 1) * group, zeros.shape[0]), :] = zeros


def apply_operator(basis_ref, blocks_ref, faces_ref, first_slot, sums_ref, buffer=None, sems=None):
    elements = blocks_ref.shape[0]
    rows = basis_ref.shape[1]
    together = TOGETHER
    steps = elements // together
    lanes = lane_ids(rows)

    def copy(step):
        return pltpu.make_async_copy(
            blocks_ref.at[pl.ds(step * together, together)], buffer.at[step % 2], sems.at[step % 2]
        )

    if buffer is not None:
        copy(0).start()

    @pl.loop(0, sums_ref.shape[0])
    def _(slot):
        sums_ref[slot] = jnp.zeros((rows, LANES), f32)

    @pl.loop(0, steps)
    def _(step):
        if buffer is not None:

            @pl.when(step + 1 < steps)
            def _():
                copy(step + 1).start()

            copy(step).wait()
        pieces = []
        for inner in range(together):
            element = step * together + inner
            left = basis_ref[faces_ref[first_slot, element]]
            right = basis_ref[faces_ref[first_slot + 1, element]]
            block = blocks_ref[element] if buffer is None else buffer[step % 2, inner]
            terms = jnp.dot(jnp.concatenate([left, right], axis=1), block, preferred_element_type=f32)
            tiles = [terms[:, LANES * n : LANES * (n + 1)] for n in range(4)]
            for slot in range(4):
                if slot == 0:
                    piece = tiles[0]
                else:
                    shift = slot * (LANES - P_SIZE)
                    piece = jnp.where(
                        lanes < shift, pltpu.roll(tiles[slot - 1], shift, 1), pltpu.roll(tiles[slot], shift, 1)
                    )
                pieces.append((faces_ref[slot, element], piece))
        for slot, piece in pieces:
            sums_ref[slot] += piece


def write_sums(sums_ref, bases, own_ref, other_ref, ghost_own_ref, ghost_other_ref):
    owned, half, _ = own_ref.shape
    rows = sums_ref.shape[1]
    ghosts = ghost_own_ref.shape[0]
    inside = lane_ids(rows) < P_SIZE

    def rounded(slot):
        return jnp.where(inside, sums_ref[slot], 0.0).astype(bf16)

    def add_dots(slot, value, dots):
        wide = value.astype(f32)
        return tuple(dot + basis[slot].astype(f32) * wide for dot, basis in zip(dots, bases))

    def owned_step(slot, dots):
        value = rounded(slot)
        own_ref[slot] = value[:half]
        other_ref[slot] = value[half:]
        return add_dots(slot, value, dots)

    def ghost_step(slot, dots):
        return add_dots(owned + slot, rounded(owned + slot), dots)

    dots = tuple(jnp.zeros((rows, LANES), f32) for _ in bases)
    dots = lax.fori_loop(0, owned, owned_step, dots, unroll=2)
    dots = lax.fori_loop(0, ghosts, ghost_step, dots, unroll=2)
    stats = stat_lanes([jnp.sum(dot, axis=1, keepdims=True) for dot in dots])

    @pl.loop(0, ghosts)
    def _(slot):
        value = jnp.where(inside, sums_ref[owned + slot], stats).astype(bf16)
        ghost_own_ref[slot] = value[:half]
        ghost_other_ref[slot] = value[half:]


def first_apply_kernel(
    ranks, entries, rhs_ref, rhs_other_ref, ghost_ref, ghost_other_ref, blocks_ref, faces_ref,
    basis_ref, own_ref, other_ref, ghost_own_out, ghost_other_out, norm_ref, sums_ref, *stream,
):
    owned, half, _ = rhs_ref.shape
    ghosts = ghost_ref.shape[0]
    inside = lane_ids(half) < P_SIZE

    def inverse_norm(ref):
        return jnp.sqrt(read_stat(gathered_block(ref, ranks), 0) / entries + epsilon)

    norm = inverse_norm(ghost_ref)
    norm_ref[...] = jnp.broadcast_to(norm, (half, LANES))
    scale = 1.0 / norm
    scale_other = 1.0 / inverse_norm(ghost_other_ref)

    @pl.loop(0, owned)
    def _(face):
        basis_ref[face] = jnp.zeros(basis_ref.shape[1:], bf16)
        basis_ref[face, :half, :P_SIZE] = (rhs_ref[face].astype(f32) * scale).astype(bf16)
        basis_ref[face, half:, :P_SIZE] = (rhs_other_ref[face].astype(f32) * scale_other).astype(bf16)

    @pl.loop(0, ghosts)
    def _(slot):
        basis_ref[owned + slot, :half] = jnp.where(inside, ghost_ref[slot].astype(f32) * scale, 0.0).astype(bf16)
        basis_ref[owned + slot, half:] = jnp.where(
            inside, ghost_other_ref[slot].astype(f32) * scale_other, 0.0
        ).astype(bf16)

    apply_operator(basis_ref, blocks_ref, faces_ref, 2 * lax.axis_index("col"), sums_ref, *stream)
    write_sums(sums_ref, [basis_ref], own_ref, other_ref, ghost_own_out, ghost_other_out)


def return_payload_kernel(stats, own_ref, other_ref, payload_ref):
    half = own_ref.shape[1]
    inside = lane_ids(half) < P_SIZE
    sums = own_ref[0].astype(f32) + other_ref[0].astype(f32)
    lanes = stat_lanes(
        [read_stat(own_ref[0].astype(f32), n) + read_stat(other_ref[0].astype(f32), n) for n in range(stats)]
    )

    @pl.loop(0, payload_ref.shape[0])
    def _(slot):
        total = own_ref[slot].astype(f32) + other_ref[slot].astype(f32)
        payload_ref[slot] = jnp.where(inside, total, lanes).astype(bf16)


def project_kernel(
    ranks, entries, own_ref, other_ref, returned_ref, basis_ref, send_ref,
    projected_ref, rounded_ref, payload_ref, diagonal_ref,
):
    owned, half, _ = own_ref.shape
    inside = lane_ids(half) < P_SIZE
    diagonal = read_stat(gathered_block(returned_ref, ranks), 0) / entries
    diagonal_ref[...] = jnp.broadcast_to(diagonal, (half, LANES))

    @pl.loop(0, owned)
    def _(face):
        projected_ref[face] = (
            own_ref[face].astype(f32)
            + other_ref[face].astype(f32)
            - diagonal * basis_ref[face, :half].astype(f32)
        )

    @pl.loop(0, payload_ref.shape[0])
    def _(slot):
        projected_ref[send_ref[0, slot]] += jnp.where(inside, returned_ref[slot].astype(f32), 0.0)

    def round_step(face, total):
        value = projected_ref[face]
        rounded_ref[face] = value.astype(bf16)
        return total + value * value

    total = lax.fori_loop(0, owned, round_step, jnp.zeros((half, LANES), f32), unroll=2)
    stats = stat_lanes([jnp.sum(total, axis=1, keepdims=True)]).astype(bf16)

    @pl.loop(0, payload_ref.shape[0])
    def _(slot):
        payload_ref[slot] = jnp.where(inside, rounded_ref[send_ref[0, slot]], stats)


def second_apply_kernel(
    ranks, entries, projected_ref, rounded_other_ref, ghost_ref, ghost_other_ref, blocks_ref, faces_ref, first_ref,
    second_ref, own_ref, other_ref, ghost_own_out, ghost_other_out, norm_ref, basis_ref, sums_ref, *stream,
):
    owned, half, _ = projected_ref.shape
    ghosts = ghost_ref.shape[0]
    inside = lane_ids(half) < P_SIZE

    def next_norm(ref):
        return jnp.sqrt(read_stat(gathered_block(ref, ranks), 0) / entries + epsilon)

    norm = next_norm(ghost_ref)
    norm_ref[...] = jnp.broadcast_to(norm, (half, LANES))
    scale = 1.0 / norm
    scale_other = 1.0 / next_norm(ghost_other_ref)

    @pl.loop(0, owned)
    def _(face):
        value = (projected_ref[face] * scale).astype(bf16)
        basis_ref[face, :half] = value
        second_ref[face] = value[:, :P_SIZE]
        basis_ref[face, half:] = (rounded_other_ref[face].astype(f32) * scale_other).astype(bf16)

    @pl.loop(0, ghosts)
    def _(slot):
        basis_ref[owned + slot, :half] = jnp.where(inside, ghost_ref[slot].astype(f32) * scale, 0.0).astype(bf16)
        basis_ref[owned + slot, half:] = jnp.where(
            inside, ghost_other_ref[slot].astype(f32) * scale_other, 0.0
        ).astype(bf16)

    apply_operator(basis_ref, blocks_ref, faces_ref, 2 * lax.axis_index("col"), sums_ref, *stream)
    write_sums(sums_ref, [first_ref, basis_ref], own_ref, other_ref, ghost_own_out, ghost_other_out)


def final_kernel(
    ranks, entries, own_ref, other_ref, returned_ref, first_ref, second_ref, send_ref, start_ref, diagonal_ref, next_ref,
    vector_ref, hessenberg_ref, image_ref,
):
    owned, half, _ = own_ref.shape
    block = gathered_block(returned_ref, ranks)
    proj_first = read_stat(block, 0) / entries
    proj_second = read_stat(block, 1) / entries

    @pl.loop(0, owned)
    def _(face):
        image_ref[face] = own_ref[face].astype(f32) + other_ref[face].astype(f32)

    @pl.loop(0, returned_ref.shape[0])
    def _(slot):
        image_ref[send_ref[0, slot]] += returned_ref[slot].astype(f32)

    @pl.loop(0, owned)
    def _(face):
        value = (
            image_ref[face][:, :P_SIZE]
            - proj_first * first_ref[face, :half, :P_SIZE].astype(f32)
            - proj_second * second_ref[face].astype(f32)
        )
        vector_ref[face] = value.astype(bf16)

    lanes = lane_ids(half)
    table = jnp.zeros((half, LANES), f32)
    for row, value in enumerate(
        [start_ref[...], diagonal_ref[...], next_ref[...], proj_first, proj_second]
    ):
        table = jnp.where(lanes == row, value, table)
    hessenberg_ref[...] = jnp.transpose(table)[: hessenberg_ref.shape[0]]


def call(kernel, out_shape, in_specs, scratch=(), limit=16, flops=0, bytes_accessed=0, **kwargs):
    return pl.pallas_call(
        kernel,
        out_shape=out_shape,
        in_specs=in_specs,
        scratch_shapes=scratch,
        compiler_params=pltpu.CompilerParams(vmem_limit_bytes=limit * MIB),
        cost_estimate=pl.CostEstimate(flops=flops, bytes_accessed=bytes_accessed, transcendentals=0),
        **kwargs,
    )


def body(adjoint_rhs, element_blocks, element_faces, send_faces):
    ranks = lax.axis_size("dom")
    rhs = jnp.transpose(adjoint_rhs, (0, 2, 1))
    owned, half, _ = rhs.shape
    entries = float(ranks * owned * P_SIZE)
    ghosts = send_faces.shape[1]
    elements, contracted, block_width = element_blocks.shape
    slots = owned + ghosts
    faces = element_faces.T
    raw = jnp.transpose(element_blocks, (1, 0, 2))
    group = 16
    rest = P_SIZE % group
    width = -(-block_width // LANES) * LANES
    work = -(-slots * 2 * half * LANES * 4 // MIB)
    spare = 5 - (-ghosts * half * LANES * 8 // MIB)

    held = elements * 2 * LANES * width * 2 + slots * 2 * half * LANES * 10
    resident = held <= 44 * MIB
    stream = []
    if not resident:
        stream = [pltpu.VMEM((2, TOGETHER, 2 * LANES, width), bf16), pltpu.SemaphoreType.DMA((2,))]
        spare += 2 * TOGETHER

    def out(shape, dtype=bf16):
        return pltpu.VMEM(shape, dtype) if resident else jax.ShapeDtypeStruct(shape, dtype)

    def swap(value):
        return lax.ppermute(value, "col", [(0, 1), (1, 0)])

    def exchange(value):
        return lax.all_to_all(value, "dom", split_axis=0, concat_axis=0, tiled=True)

    rhs_other = swap(rhs)

    payload = call(first_payload_kernel, out((ghosts, half, LANES)), [VMEM, SMEM])(rhs, send_faces)
    ghost = exchange(payload)

    row = jnp.arange(group * group)
    column = jnp.arange(group * group)
    perm = ((row[:, None] // group == column[None, :] % group) & (row[:, None] % group == column[None, :] // group))
    perm = perm.astype(bf16)
    tail = perm[:, : rest * group]
    blocks = call(
        relayout_kernel,
        out((elements, 2 * LANES, width)),
        [ANY, VMEM, VMEM],
        [pltpu.VMEM((2, contracted, group, block_width), bf16), pltpu.SemaphoreType.DMA((2,))],
        limit=14 if resident else 40,
        flops=2 * 256 * 256 * 512 * 84,
        bytes_accessed=2 * raw.size,
    )(raw, perm, tail)
    if resident:
        blocks = pltpu.with_memory_space_constraint(blocks, pltpu.VMEM)
    held_blocks = VMEM if resident else ANY

    ghost_other = swap(ghost)

    field = out((owned, half, LANES))
    ghost_field = out((ghosts, half, LANES))
    column_values = out((half, LANES), f32)
    sums = pltpu.VMEM((slots, 2 * half, LANES), f32)
    first_basis, own, other, ghost_own, ghost_cross, start_norm = call(
        functools.partial(first_apply_kernel, ranks, entries),
        (out((slots, 2 * half, LANES)), field, field, ghost_field, ghost_field, column_values),
        [VMEM] * 4 + [held_blocks, SMEM],
        [sums] + stream,
        limit=work + spare,
    )(rhs, rhs_other, ghost, ghost_other, blocks, faces)

    ghost_cross = swap(ghost_cross)
    other = swap(other)
    payload = call(functools.partial(return_payload_kernel, 1), ghost_field, [VMEM, VMEM])(ghost_own, ghost_cross)
    returned = exchange(payload)

    projected, rounded, payload, diagonal = call(
        functools.partial(project_kernel, ranks, entries),
        (out((owned, half, LANES), f32), field, ghost_field, column_values),
        [VMEM] * 4 + [SMEM],
    )(own, other, returned, first_basis, send_faces)

    rounded_other = swap(rounded)
    ghost = exchange(payload)
    ghost_other = swap(ghost)

    second, own, other, ghost_own, ghost_cross, next_norm = call(
        functools.partial(second_apply_kernel, ranks, entries),
        (out((owned, half, P_SIZE)), field, field, ghost_field, ghost_field, column_values),
        [VMEM] * 4 + [held_blocks, SMEM, VMEM],
        [pltpu.VMEM((slots, 2 * half, LANES), bf16), sums] + stream,
        limit=work + work // 2 + spare,
    )(projected, rounded_other, ghost, ghost_other, blocks, faces, first_basis)

    ghost_cross = swap(ghost_cross)
    other = swap(other)
    payload = call(functools.partial(return_payload_kernel, 2), ghost_field, [VMEM, VMEM])(ghost_own, ghost_cross)
    returned = exchange(payload)

    vector, hessenberg = call(
        functools.partial(final_kernel, ranks, entries),
        (jax.ShapeDtypeStruct((owned, half, P_SIZE), bf16), jax.ShapeDtypeStruct((5, half), f32)),
        [VMEM] * 5 + [SMEM] + [VMEM] * 3,
        [pltpu.VMEM((owned, half, LANES), f32)],
    )(own, other, returned, first_basis, second, send_faces, start_norm, diagonal, next_norm)

    return (jnp.transpose(second, (0, 2, 1)), jnp.transpose(vector, (0, 2, 1)), hessenberg)


def solution(mesh):
    in_specs = (P("dom", None, "col"), P("dom", "col", None), P("dom", None), P("dom", None))
    out_specs = (P("dom", None, "col"), P("dom", None, "col"), P(None, "col"))
    return jax.shard_map(body, mesh=mesh, in_specs=in_specs, out_specs=out_specs, check_vma=False)
```

```python
import functools

import jax
import jax.numpy as jnp
from jax import lax
from jax.experimental import pallas as pl
from jax.experimental.pallas import tpu as pltpu
from jax.sharding import PartitionSpec as P

P_SIZE = 105
LANES = 128
MIB = 1 << 20
TOGETHER = 32

epsilon = 1e-06

f32 = jnp.float32
bf16 = jnp.bfloat16

VMEM = pl.BlockSpec(memory_space=pltpu.VMEM)
SMEM = pl.BlockSpec(memory_space=pltpu.SMEM)
ANY = pl.BlockSpec(memory_space=pl.ANY)
HBM = pl.BlockSpec(memory_space=pltpu.HBM)


def lane_ids(rows):
    return lax.broadcasted_iota(jnp.int32, (rows, LANES), 1)


def stat_lanes(columns):
    rows = columns[0].shape[0]
    lanes = lane_ids(rows)
    block = jnp.zeros((rows, LANES), f32)
    lane = P_SIZE
    for value in columns:
        rest = value * 0.5
        for _ in range(3):
            part = rest.astype(bf16).astype(f32)
            block = jnp.where(lanes == lane, part, block)
            rest = rest - part
            lane += 1
    return block


def read_stat(block, which):
    lanes = lane_ids(block.shape[0])
    first = P_SIZE + 3 * which
    inside = (lanes >= first) & (lanes < first + 3)
    return 2.0 * jnp.sum(jnp.where(inside, block, 0.0), axis=1, keepdims=True)


def gathered_block(ghost_ref, ranks):
    slots = ghost_ref.shape[0] // ranks
    total = ghost_ref[0].astype(f32)
    for rank in range(1, ranks):
        total = total + ghost_ref[rank * slots].astype(f32)
    return total


def first_payload_kernel(rhs_ref, send_ref, payload_ref):
    faces, rows, _ = rhs_ref.shape

    def add(face, total):
        value = rhs_ref[face].astype(f32)
        return total + value * value

    total = lax.fori_loop(0, faces, add, jnp.zeros((rows, P_SIZE), f32), unroll=8)
    stats = stat_lanes([jnp.sum(total, axis=1, keepdims=True)]).astype(bf16)

    @pl.loop(0, payload_ref.shape[0], unroll=4)
    def _(slot):
        payload_ref[slot] = stats
        payload_ref[slot, :, :P_SIZE] = rhs_ref[send_ref[0, slot]]


def relayout(source, perm_ref, tail_ref, target):
    group = source.shape[1]
    width = source.shape[2]
    full = P_SIZE // group
    rest = P_SIZE - full * group
    for slot in range(source.shape[0] // P_SIZE):
        for part in range(full + 1):
            first = slot * P_SIZE + part * group
            depth = group if part < full else rest
            chunk = source[first : first + depth].reshape(depth * group, width)
            perm = perm_ref[...] if part < full else tail_ref[...]
            moved = jnp.dot(perm, chunk, preferred_element_type=f32).astype(bf16)
            for element in range(group):
                target[element, pl.ds(slot * LANES + part * group, group), :width] = moved[
                    element * group : (element + 1) * group
                ]
        zeros = jnp.zeros((LANES - (full + 1) * group, target.shape[2]), bf16)
        for element in range(group):
            target[element, pl.ds(slot * LANES + (full + 1) * group, zeros.shape[0]), :] = zeros


def copy_group(source_ref, buffer, sems, step):
    group = buffer.shape[2]
    return pltpu.make_async_copy(
        source_ref.at[:, pl.ds(step * group, group), :], buffer.at[step % 2], sems.at[step % 2]
    )


def relayout_kernel(raw_ref, perm_ref, tail_ref, out_ref, buffer, staging, sems, out_sems):
    group = buffer.shape[2]
    steps = raw_ref.shape[1] // group

    def copy_out(step):
        return pltpu.make_async_copy(
            staging.at[step % 2], out_ref.at[pl.ds(step * group, group)], out_sems.at[step % 2]
        )

    copy_group(raw_ref, buffer, sems, 0).start()
    for step in range(steps):
        if step + 1 < steps:
            copy_group(raw_ref, buffer, sems, step + 1).start()
        copy_group(raw_ref, buffer, sems, step).wait()
        if step >= 2:
            copy_out(step - 2).wait()
        relayout(buffer.at[step % 2], perm_ref, tail_ref, staging.at[step % 2])
        copy_out(step).start()
    for step in range(max(0, steps - 2), steps):
        copy_out(step).wait()


def slot_pieces(terms):
    lanes = lane_ids(terms.shape[0])
    tiles = [terms[:, LANES * n : LANES * (n + 1)] for n in range(4)]
    pieces = [tiles[0]]
    for slot in range(1, 4):
        shift = slot * (LANES - P_SIZE)
        pieces.append(
            jnp.where(lanes < shift, pltpu.roll(tiles[slot - 1], shift, 1), pltpu.roll(tiles[slot], shift, 1))
        )
    return pieces


def add_terms(first, blocks, basis_ref, faces_ref, first_slot, sums_ref):
    pieces = []
    for inner, block in enumerate(blocks):
        left = basis_ref[faces_ref[first_slot, first + inner]]
        right = basis_ref[faces_ref[first_slot + 1, first + inner]]
        terms = jnp.dot(jnp.concatenate([left, right], axis=1), block(), preferred_element_type=f32)
        for slot, piece in enumerate(slot_pieces(terms)):
            pieces.append((faces_ref[slot, first + inner], piece))
    for slot, piece in pieces:
        sums_ref[slot] += piece


def held_apply(blocks_refs, *refs):
    first = 0
    for blocks_ref in blocks_refs:
        count = blocks_ref.shape[0]
        together = max(n for n in range(1, TOGETHER + 1) if count % n == 0)

        @pl.loop(0, count // together)
        def _(step, blocks_ref=blocks_ref, first=first, together=together):
            at = step * together
            add_terms(first + at, [lambda n=n: blocks_ref[at + n] for n in range(together)], *refs)

        first += count


def streamed_apply(blocks_ref, buffer, sems, *refs):
    group = buffer.shape[1]
    steps = blocks_ref.shape[0] // group

    def copy(step):
        return pltpu.make_async_copy(
            blocks_ref.at[pl.ds(step * group, group)], buffer.at[step % 2], sems.at[step % 2]
        )

    copy(0).start()
    for step in range(steps):
        if step + 1 < steps:
            copy(step + 1).start()
        copy(step).wait()
        add_terms(step * group, [lambda n=n: buffer[step % 2, n] for n in range(group)], *refs)


def relayout_apply(raw_ref, perm_ref, tail_ref, blocks_refs, buffer, sems, *refs):
    group = buffer.shape[2]
    targets = [
        (blocks_ref, first) for blocks_ref in blocks_refs for first in range(0, blocks_ref.shape[0], group)
    ]
    for step, (target, first) in enumerate(targets):
        copy_group(raw_ref, buffer, sems, step).wait()
        relayout(buffer.at[step % 2], perm_ref, tail_ref, target.at[pl.ds(first, group)])
        if step + 2 < len(targets):
            copy_group(raw_ref, buffer, sems, step + 2).start()
        add_terms(step * group, [lambda n=n: target[first + n] for n in range(group)], *refs)


def masked_sum(value):
    return jnp.sum(jnp.where(lane_ids(value.shape[0]) < P_SIZE, value, 0.0), axis=1, keepdims=True)


def slot_loop(first, last, step, carry):
    return lax.fori_loop(first, last, step, carry, unroll=4)


def ghost_lanes(sums_ref, stats, ghost_own_out, ghost_other_out):
    ghosts, half, _ = ghost_own_out.shape
    owned = sums_ref.shape[0] - ghosts
    inside = lane_ids(2 * half) < P_SIZE

    @pl.loop(0, ghosts, unroll=4)
    def _(slot):
        value = jnp.where(inside, sums_ref[owned + slot], stats).astype(bf16)
        ghost_own_out[slot] = value[:half]
        ghost_other_out[slot] = value[half:]


def norm_of(ghost_ref, ranks, entries):
    return jnp.sqrt(read_stat(gathered_block(ghost_ref, ranks), 0) / entries + epsilon)


def fill_ghosts(basis_ref, sums_ref, ghost_ref, ghost_other_ref, scale, scale_other):
    ghosts, half, _ = ghost_ref.shape
    owned = sums_ref.shape[0] - ghosts
    inside = lane_ids(half) < P_SIZE

    @pl.loop(0, ghosts, unroll=4)
    def _(slot):
        sums_ref[owned + slot] = jnp.zeros((2 * half, LANES), f32)
        basis_ref[owned + slot, :half] = jnp.where(inside, ghost_ref[slot].astype(f32) * scale, 0.0).astype(bf16)
        basis_ref[owned + slot, half:] = jnp.where(
            inside, ghost_other_ref[slot].astype(f32) * scale_other, 0.0
        ).astype(bf16)


def first_apply_kernel(
    ranks, entries, fused, rhs_ref, rhs_other_ref, ghost_ref, ghost_other_ref, faces_ref, *refs,
):
    owned, half, _ = rhs_ref.shape
    ghosts = ghost_ref.shape[0]
    rows = 2 * half
    if fused:
        raw_ref, perm_ref, tail_ref, *outs, buffer, sems = refs
        blocks_refs = outs[5:]
        for step in range(2):
            copy_group(raw_ref, buffer, sems, step).start()
    else:
        blocks_ref, *outs, buffer, sems = refs
    basis_ref, sums_ref, ghost_own_out, ghost_other_out, norm_ref = outs[:5]

    norm = norm_of(ghost_ref, ranks, entries)
    norm_ref[...] = jnp.broadcast_to(norm, (half, LANES))
    scale = 1.0 / norm
    scale_other = 1.0 / norm_of(ghost_other_ref, ranks, entries)

    @pl.loop(0, owned, unroll=4)
    def _(face):
        sums_ref[face] = jnp.zeros((rows, LANES), f32)
        basis_ref[face] = jnp.zeros((rows, LANES), bf16)
        basis_ref[face, :half, :P_SIZE] = (rhs_ref[face].astype(f32) * scale).astype(bf16)
        basis_ref[face, half:, :P_SIZE] = (rhs_other_ref[face].astype(f32) * scale_other).astype(bf16)

    fill_ghosts(basis_ref, sums_ref, ghost_ref, ghost_other_ref, scale, scale_other)
    field = (basis_ref, faces_ref, 2 * lax.axis_index("col"), sums_ref)
    if fused:
        relayout_apply(raw_ref, perm_ref, tail_ref, blocks_refs, buffer, sems, *field)
    else:
        streamed_apply(blocks_ref, buffer, sems, *field)

    def dot_step(slot, dot):
        return dot + basis_ref[slot].astype(f32) * sums_ref[slot]

    dot = slot_loop(0, owned + ghosts, dot_step, jnp.zeros((rows, LANES), f32))
    ghost_lanes(sums_ref, stat_lanes([masked_sum(dot)]), ghost_own_out, ghost_other_out)


def fields_kernel(sums_ref, own_ref, other_ref):
    owned, half, _ = own_ref.shape

    @pl.loop(0, owned, unroll=4)
    def _(slot):
        value = sums_ref[slot].astype(bf16)
        own_ref[slot] = value[:half]
        other_ref[slot] = value[half:]


def return_payload_kernel(stats, own_ref, other_ref, sums_ref, payload_ref, same_sums_ref):
    del sums_ref, same_sums_ref
    half = own_ref.shape[1]
    inside = lane_ids(half) < P_SIZE
    own = own_ref[0].astype(f32)
    other = other_ref[0].astype(f32)
    lanes = stat_lanes([read_stat(own, n) + read_stat(other, n) for n in range(stats)])

    @pl.loop(0, payload_ref.shape[0], unroll=4)
    def _(slot):
        total = own_ref[slot].astype(f32) + other_ref[slot].astype(f32)
        payload_ref[slot] = jnp.where(inside, total, lanes).astype(bf16)


def project_kernel(
    ranks, entries, own_ref, other_ref, returned_ref, basis_ref, send_ref,
    rounded_ref, payload_ref, diagonal_ref, projected_ref,
):
    owned, half, _ = own_ref.shape
    ghosts = payload_ref.shape[0]
    inside = lane_ids(half) < P_SIZE
    diagonal = read_stat(gathered_block(returned_ref, ranks), 0) / entries
    diagonal_ref[...] = jnp.broadcast_to(diagonal, (half, LANES))

    @pl.loop(0, owned, unroll=4)
    def _(face):
        projected_ref[face] = (
            own_ref[face].astype(f32)
            + other_ref[face].astype(f32)
            - diagonal * basis_ref[face, :half].astype(f32)
        )

    @pl.loop(0, ghosts)
    def _(slot):
        projected_ref[send_ref[0, slot]] += returned_ref[slot].astype(f32)

    def round_step(face, total):
        value = projected_ref[face]
        rounded_ref[face] = value.astype(bf16)
        return total + value * value

    total = slot_loop(0, owned, round_step, jnp.zeros((half, LANES), f32))
    stats = stat_lanes([masked_sum(total)]).astype(bf16)

    @pl.loop(0, ghosts, unroll=4)
    def _(slot):
        payload_ref[slot] = jnp.where(inside, rounded_ref[send_ref[0, slot]], stats)


def second_apply_kernel(
    ranks, entries, held, rounded_ref, rounded_other_ref, ghost_ref, ghost_other_ref, faces_ref, first_ref, spent_ref,
    *refs,
):
    del spent_ref
    stream = [] if held else refs[-2:]
    refs = refs if held else refs[:-2]
    *blocks_refs, basis_ref, sums_ref, ghost_own_out, ghost_other_out, norm_ref, second_ref, staging, out_sem = refs
    owned, half, _ = rounded_ref.shape
    ghosts = ghost_ref.shape[0]
    rows = 2 * half
    norm = norm_of(ghost_ref, ranks, entries)
    norm_ref[...] = jnp.broadcast_to(norm, (half, LANES))
    scale = 1.0 / norm
    scale_other = 1.0 / norm_of(ghost_other_ref, ranks, entries)

    @pl.loop(0, owned, unroll=4)
    def _(face):
        sums_ref[face] = jnp.zeros((rows, LANES), f32)
        value = (rounded_ref[face].astype(f32) * scale).astype(bf16)
        basis_ref[face, :half] = value
        staging[face] = value[:, :P_SIZE]
        basis_ref[face, half:] = (rounded_other_ref[face].astype(f32) * scale_other).astype(bf16)

    out_copy = pltpu.make_async_copy(staging, second_ref, out_sem)
    out_copy.start()
    fill_ghosts(basis_ref, sums_ref, ghost_ref, ghost_other_ref, scale, scale_other)
    field = (basis_ref, faces_ref, 2 * lax.axis_index("col"), sums_ref)
    if held:
        held_apply(blocks_refs, *field)
    else:
        streamed_apply(blocks_refs[0], *stream, *field)

    def dot_step(slot, dots):
        value = sums_ref[slot]
        return tuple(dot + basis[slot].astype(f32) * value for dot, basis in zip(dots, (first_ref, basis_ref)))

    zeros = jnp.zeros((rows, LANES), f32)
    dots = slot_loop(0, owned + ghosts, dot_step, (zeros, zeros))
    ghost_lanes(sums_ref, stat_lanes([masked_sum(dot) for dot in dots]), ghost_own_out, ghost_other_out)
    out_copy.wait()


def final_kernel(
    ranks, entries, own_ref, other_ref, returned_ref, first_ref, second_ref, send_ref, start_ref, diagonal_ref, next_ref,
    vector_ref, hessenberg_ref, image_ref,
):
    owned, half, _ = own_ref.shape
    block = gathered_block(returned_ref, ranks)
    proj_first = read_stat(block, 0) / entries
    proj_second = read_stat(block, 1) / entries

    @pl.loop(0, owned, unroll=4)
    def _(face):
        value = (
            own_ref[face].astype(f32)
            + other_ref[face].astype(f32)
            - proj_first * first_ref[face, :half].astype(f32)
        )
        image_ref[face] = value - proj_second * second_ref[face, :half].astype(f32)

    @pl.loop(0, returned_ref.shape[0])
    def _(slot):
        image_ref[send_ref[0, slot]] += returned_ref[slot].astype(f32)

    @pl.loop(0, owned, unroll=4)
    def _(face):
        vector_ref[face] = image_ref[face, :, :P_SIZE].astype(bf16)

    lanes = lane_ids(half)
    table = jnp.zeros((half, LANES), f32)
    for row, value in enumerate(
        [start_ref[...], diagonal_ref[...], next_ref[...], proj_first, proj_second]
    ):
        table = jnp.where(lanes == row, value, table)
    hessenberg_ref[...] = jnp.transpose(table)[: hessenberg_ref.shape[0]]


def call(kernel, out_shape, in_specs, scratch=(), limit=16, flops=0, bytes_accessed=0, **kwargs):
    return pl.pallas_call(
        kernel,
        out_shape=out_shape,
        in_specs=in_specs,
        scratch_shapes=scratch,
        compiler_params=pltpu.CompilerParams(vmem_limit_bytes=limit * MIB),
        cost_estimate=pl.CostEstimate(flops=flops, bytes_accessed=bytes_accessed, transcendentals=0),
        **kwargs,
    )


def body(adjoint_rhs, element_blocks, element_faces, send_faces):
    ranks = lax.axis_size("dom")
    rhs = jnp.transpose(adjoint_rhs, (0, 2, 1))
    owned, half, _ = rhs.shape
    entries = float(ranks * owned * P_SIZE)
    ghosts = send_faces.shape[1]
    elements, contracted, block_width = element_blocks.shape
    slots = owned + ghosts
    faces = element_faces.T
    raw = jnp.transpose(element_blocks, (1, 0, 2))
    group = 16
    rest = P_SIZE % group
    width = -(-block_width // LANES) * LANES
    sums_bytes = slots * 2 * half * LANES * 4
    resident = elements * 2 * LANES * width * 2 + 3 * sums_bytes <= 48 * MIB

    def out(shape, dtype=bf16):
        return pltpu.VMEM(shape, dtype) if resident else jax.ShapeDtypeStruct(shape, dtype)

    stream = [pltpu.VMEM((2, group, 2 * LANES, width), bf16), pltpu.SemaphoreType.DMA((2,))]

    def limit(amount):
        return amount if resident else 50

    def swap(value):
        return lax.ppermute(value, "col", [(0, 1), (1, 0)])

    def exchange(value):
        return lax.all_to_all(value, "dom", split_axis=0, concat_axis=0, tiled=True)

    rhs_other = swap(rhs)

    ghost_field = out((ghosts, half, LANES))
    payload = call(first_payload_kernel, ghost_field, [VMEM, SMEM], limit=limit(4))(rhs, send_faces)
    ghost = exchange(payload)

    row = jnp.arange(group * group)
    column = jnp.arange(group * group)
    perm = ((row[:, None] // group == column[None, :] % group) & (row[:, None] % group == column[None, :] // group))
    perm = perm.astype(bf16)
    tail = perm[:, : rest * group]
    raw_buffer = [pltpu.VMEM((2, contracted, group, block_width), bf16), pltpu.SemaphoreType.DMA((2,))]
    blocks_shape = (elements, 2 * LANES, width)
    parts = elements // (2 * group) if resident and elements % (2 * group) == 0 else 1
    if resident:
        operands = (raw, perm, tail)
    else:
        blocks = call(
            relayout_kernel,
            jax.ShapeDtypeStruct(blocks_shape, bf16),
            [HBM, VMEM, VMEM],
            [raw_buffer[0], stream[0], raw_buffer[1], stream[1]],
            limit=limit(20),
            out_specs=HBM,
        )(raw, perm, tail)
        operands = (blocks,)

    ghost_other = swap(ghost)

    field = out((owned, half, LANES))
    basis = out((slots, 2 * half, LANES))
    sums_field = out((slots, 2 * half, LANES), f32)
    column_values = out((half, LANES), f32)
    outs = (basis, sums_field, ghost_field, ghost_field, column_values)
    first_basis, sums, ghost_own, ghost_cross, start_norm, *blocks_held = call(
        functools.partial(first_apply_kernel, ranks, entries, resident),
        outs + ((out((elements // parts, *blocks_shape[1:])),) * parts if resident else ()),
        [VMEM] * 4 + [SMEM] + ([HBM, VMEM, VMEM] if resident else [HBM]),
        raw_buffer if resident else stream,
        limit=limit(12),
    )(rhs, rhs_other, ghost, ghost_other, faces, *operands)
    blocks = blocks_held if resident else [blocks]

    def return_payload(stats, ghost_own, ghost_cross, sums):
        return call(
            functools.partial(return_payload_kernel, stats), (ghost_field, sums_field),
            [VMEM, VMEM, ANY], limit=limit(4), input_output_aliases={2: 1}, out_specs=(VMEM, ANY),
        )(ghost_own, ghost_cross, sums)

    payload, sums = return_payload(1, ghost_own, swap(ghost_cross), sums)
    returned = exchange(payload)
    own, other = call(fields_kernel, (field, field), [VMEM], limit=limit(4))(sums)
    other = swap(other)

    rounded, payload, diagonal = call(
        functools.partial(project_kernel, ranks, entries),
        (field, ghost_field, column_values),
        [VMEM] * 4 + [SMEM],
        [pltpu.VMEM((owned, half, LANES), f32)],
        limit=limit(8),
    )(own, other, returned, first_basis, send_faces)

    rounded_other = swap(rounded)
    ghost = exchange(payload)
    ghost_other = swap(ghost)
    second_basis, sums, ghost_own, ghost_cross, next_norm, second = call(
        functools.partial(second_apply_kernel, ranks, entries, resident),
        outs + (jax.ShapeDtypeStruct((owned, half, P_SIZE), bf16),),
        [VMEM] * 4 + [SMEM, VMEM, ANY] + [VMEM if resident else HBM] * len(blocks),
        [pltpu.VMEM((owned, half, P_SIZE), bf16), pltpu.SemaphoreType.DMA] + ([] if resident else stream),
        limit=limit(6),
        out_specs=(VMEM,) * 5 + (HBM,),
        input_output_aliases={6: 1},
    )(rounded, rounded_other, ghost, ghost_other, faces, first_basis, sums, *blocks)

    payload, sums = return_payload(2, ghost_own, swap(ghost_cross), sums)
    returned = exchange(payload)
    own, other = call(fields_kernel, (field, field), [VMEM], limit=limit(4))(sums)
    other = swap(other)

    vector, hessenberg = call(
        functools.partial(final_kernel, ranks, entries),
        (jax.ShapeDtypeStruct((owned, half, P_SIZE), bf16), jax.ShapeDtypeStruct((5, half), f32)),
        [VMEM] * 5 + [SMEM] + [VMEM] * 3,
        [pltpu.VMEM((owned, half, LANES), f32)],
        limit=limit(10),
    )(own, other, returned, first_basis, second_basis, send_faces, start_norm, diagonal, next_norm)

    return (jnp.transpose(second, (0, 2, 1)), jnp.transpose(vector, (0, 2, 1)), hessenberg)


def solution(mesh):
    in_specs = (P("dom", None, "col"), P("dom", "col", None), P("dom", None), P("dom", None))
    out_specs = (P("dom", None, "col"), P("dom", None, "col"), P(None, "col"))
    return jax.shard_map(body, mesh=mesh, in_specs=in_specs, out_specs=out_specs, check_vma=False)
```

```python
import functools

import jax
import jax.numpy as jnp
from jax import lax
from jax.experimental import pallas as pl
from jax.experimental.pallas import tpu as pltpu
from jax.sharding import PartitionSpec as P

P_SIZE = 105
LANES = 128
MIB = 1 << 20
TOGETHER = 32

epsilon = 1e-06

f32 = jnp.float32
bf16 = jnp.bfloat16

VMEM = pl.BlockSpec(memory_space=pltpu.VMEM)
SMEM = pl.BlockSpec(memory_space=pltpu.SMEM)
ANY = pl.BlockSpec(memory_space=pl.ANY)
HBM = pl.BlockSpec(memory_space=pltpu.HBM)


def lane_ids(rows):
    return lax.broadcasted_iota(jnp.int32, (rows, LANES), 1)


def stat_lanes(columns):
    rows = columns[0].shape[0]
    lanes = lane_ids(rows)
    block = jnp.zeros((rows, LANES), f32)
    lane = P_SIZE
    for value in columns:
        rest = value * 0.5
        for _ in range(3):
            part = rest.astype(bf16).astype(f32)
            block = jnp.where(lanes == lane, part, block)
            rest = rest - part
            lane += 1
    return block


def read_stat(block, which):
    lanes = lane_ids(block.shape[0])
    first = P_SIZE + 3 * which
    inside = (lanes >= first) & (lanes < first + 3)
    return 2.0 * jnp.sum(jnp.where(inside, block, 0.0), axis=1, keepdims=True)


def gathered_block(ghost_ref, ranks):
    slots = ghost_ref.shape[0] // ranks
    total = ghost_ref[0].astype(f32)
    for rank in range(1, ranks):
        total = total + ghost_ref[rank * slots].astype(f32)
    return total


def first_payload_kernel(rhs_ref, send_ref, payload_ref):
    faces, rows, _ = rhs_ref.shape

    def add(face, total):
        value = rhs_ref[face].astype(f32)
        return total + value * value

    total = lax.fori_loop(0, faces, add, jnp.zeros((rows, P_SIZE), f32), unroll=8)
    stats = stat_lanes([jnp.sum(total, axis=1, keepdims=True)]).astype(bf16)

    @pl.loop(0, payload_ref.shape[0], unroll=4)
    def _(slot):
        payload_ref[slot] = stats
        payload_ref[slot, :, :P_SIZE] = rhs_ref[send_ref[0, slot]]


def relayout(source, perm_ref, tail_ref, target):
    group = source.shape[1]
    width = source.shape[2]
    full = P_SIZE // group
    rest = P_SIZE - full * group
    for slot in range(source.shape[0] // P_SIZE):
        for part in range(full + 1):
            first = slot * P_SIZE + part * group
            depth = group if part < full else rest
            chunk = source[first : first + depth].reshape(depth * group, width)
            perm = perm_ref[...] if part < full else tail_ref[...]
            moved = jnp.dot(perm, chunk, preferred_element_type=f32).astype(bf16)
            for element in range(group):
                target[element, pl.ds(slot * LANES + part * group, group), :width] = moved[
                    element * group : (element + 1) * group
                ]
        zeros = jnp.zeros((LANES - (full + 1) * group, target.shape[2]), bf16)
        for element in range(group):
            target[element, pl.ds(slot * LANES + (full + 1) * group, zeros.shape[0]), :] = zeros


def copy_group(source_ref, buffer, sems, step):
    group = buffer.shape[2]
    return pltpu.make_async_copy(
        source_ref.at[:, pl.ds(step * group, group), :], buffer.at[step % 2], sems.at[step % 2]
    )


def relayout_kernel(raw_ref, perm_ref, tail_ref, out_ref, buffer, staging, sems, out_sems):
    group = buffer.shape[2]
    steps = raw_ref.shape[1] // group

    def copy_out(step):
        return pltpu.make_async_copy(
            staging.at[step % 2], out_ref.at[pl.ds(step * group, group)], out_sems.at[step % 2]
        )

    copy_group(raw_ref, buffer, sems, 0).start()
    for step in range(steps):
        if step + 1 < steps:
            copy_group(raw_ref, buffer, sems, step + 1).start()
        copy_group(raw_ref, buffer, sems, step).wait()
        if step >= 2:
            copy_out(step - 2).wait()
        relayout(buffer.at[step % 2], perm_ref, tail_ref, staging.at[step % 2])
        copy_out(step).start()
    for step in range(max(0, steps - 2), steps):
        copy_out(step).wait()


def slot_pieces(terms):
    lanes = lane_ids(terms.shape[0])
    tiles = [terms[:, LANES * n : LANES * (n + 1)] for n in range(4)]
    pieces = [tiles[0]]
    for slot in range(1, 4):
        shift = slot * (LANES - P_SIZE)
        pieces.append(
            jnp.where(lanes < shift, pltpu.roll(tiles[slot - 1], shift, 1), pltpu.roll(tiles[slot], shift, 1))
        )
    return pieces


def add_terms(first, blocks, basis_ref, faces_ref, first_slot, sums_ref):
    pieces = []
    for inner, block in enumerate(blocks):
        left = basis_ref[faces_ref[first_slot, first + inner]]
        right = basis_ref[faces_ref[first_slot + 1, first + inner]]
        terms = jnp.dot(jnp.concatenate([left, right], axis=1), block(), preferred_element_type=f32)
        for slot, piece in enumerate(slot_pieces(terms)):
            pieces.append((faces_ref[slot, first + inner], piece))
    for slot, piece in pieces:
        sums_ref[slot] += piece


def held_apply(blocks_refs, *refs):
    first = 0
    for blocks_ref in blocks_refs:
        count = blocks_ref.shape[0]
        together = max(n for n in range(1, TOGETHER + 1) if count % n == 0)

        @pl.loop(0, count // together)
        def _(step, blocks_ref=blocks_ref, first=first, together=together):
            at = step * together
            add_terms(first + at, [lambda n=n: blocks_ref[at + n] for n in range(together)], *refs)

        first += count


def streamed_apply(blocks_ref, buffer, sems, *refs):
    group = buffer.shape[1]
    steps = blocks_ref.shape[0] // group

    def copy(step):
        return pltpu.make_async_copy(
            blocks_ref.at[pl.ds(step * group, group)], buffer.at[step % 2], sems.at[step % 2]
        )

    copy(0).start()
    for step in range(steps):
        if step + 1 < steps:
            copy(step + 1).start()
        copy(step).wait()
        add_terms(step * group, [lambda n=n: buffer[step % 2, n] for n in range(group)], *refs)


def relayout_apply(raw_ref, perm_ref, tail_ref, blocks_refs, buffer, sems, *refs):
    group = buffer.shape[2]
    targets = [
        (blocks_ref, first) for blocks_ref in blocks_refs for first in range(0, blocks_ref.shape[0], group)
    ]
    def apply_step(step):
        target, first = targets[step]
        add_terms(step * group, [lambda n=n: target[first + n] for n in range(group)], *refs)

    for step, (target, first) in enumerate(targets):
        copy_group(raw_ref, buffer, sems, step).wait()
        relayout(buffer.at[step % 2], perm_ref, tail_ref, target.at[pl.ds(first, group)])
        if step:
            apply_step(step - 1)
        if step + 2 < len(targets):
            copy_group(raw_ref, buffer, sems, step + 2).start()
    apply_step(len(targets) - 1)


def masked_sum(value):
    return jnp.sum(jnp.where(lane_ids(value.shape[0]) < P_SIZE, value, 0.0), axis=1, keepdims=True)


def slot_loop(first, last, step, carry):
    return lax.fori_loop(first, last, step, carry, unroll=4)


def ghost_lanes(sums_ref, stats, ghost_own_out, ghost_other_out):
    ghosts, half, _ = ghost_own_out.shape
    owned = sums_ref.shape[0] - ghosts
    inside = lane_ids(2 * half) < P_SIZE

    @pl.loop(0, ghosts, unroll=4)
    def _(slot):
        value = jnp.where(inside, sums_ref[owned + slot], stats).astype(bf16)
        ghost_own_out[slot] = value[:half]
        ghost_other_out[slot] = value[half:]


def norm_of(ghost_ref, ranks, entries):
    return jnp.sqrt(read_stat(gathered_block(ghost_ref, ranks), 0) / entries + epsilon)


def fill_ghosts(basis_ref, sums_ref, ghost_ref, ghost_other_ref, scale, scale_other):
    ghosts, half, _ = ghost_ref.shape
    owned = sums_ref.shape[0] - ghosts
    inside = lane_ids(half) < P_SIZE

    @pl.loop(0, ghosts, unroll=4)
    def _(slot):
        sums_ref[owned + slot] = jnp.zeros((2 * half, LANES), f32)
        basis_ref[owned + slot, :half] = jnp.where(inside, ghost_ref[slot].astype(f32) * scale, 0.0).astype(bf16)
        basis_ref[owned + slot, half:] = jnp.where(
            inside, ghost_other_ref[slot].astype(f32) * scale_other, 0.0
        ).astype(bf16)


def first_apply_kernel(
    ranks, entries, fused, rhs_ref, rhs_other_ref, ghost_ref, ghost_other_ref, faces_ref, *refs,
):
    owned, half, _ = rhs_ref.shape
    ghosts = ghost_ref.shape[0]
    rows = 2 * half
    if fused:
        raw_ref, perm_ref, tail_ref, *outs, buffer, sems = refs
        blocks_refs = outs[5:]
        for step in range(2):
            copy_group(raw_ref, buffer, sems, step).start()
    else:
        blocks_ref, *outs, buffer, sems = refs
    basis_ref, sums_ref, ghost_own_out, ghost_other_out, norm_ref = outs[:5]

    norm = norm_of(ghost_ref, ranks, entries)
    norm_ref[...] = jnp.broadcast_to(norm, (half, LANES))
    scale = 1.0 / norm
    scale_other = 1.0 / norm_of(ghost_other_ref, ranks, entries)

    @pl.loop(0, owned, unroll=4)
    def _(face):
        sums_ref[face] = jnp.zeros((rows, LANES), f32)
        basis_ref[face] = jnp.zeros((rows, LANES), bf16)
        basis_ref[face, :half, :P_SIZE] = (rhs_ref[face].astype(f32) * scale).astype(bf16)
        basis_ref[face, half:, :P_SIZE] = (rhs_other_ref[face].astype(f32) * scale_other).astype(bf16)

    fill_ghosts(basis_ref, sums_ref, ghost_ref, ghost_other_ref, scale, scale_other)
    field = (basis_ref, faces_ref, 2 * lax.axis_index("col"), sums_ref)
    if fused:
        relayout_apply(raw_ref, perm_ref, tail_ref, blocks_refs, buffer, sems, *field)
    else:
        streamed_apply(blocks_ref, buffer, sems, *field)

    def dot_step(slot, dot):
        return dot + basis_ref[slot].astype(f32) * sums_ref[slot]

    dot = slot_loop(0, owned + ghosts, dot_step, jnp.zeros((rows, LANES), f32))
    ghost_lanes(sums_ref, stat_lanes([masked_sum(dot)]), ghost_own_out, ghost_other_out)


def fields_kernel(sums_ref, own_ref, other_ref):
    owned, half, _ = own_ref.shape

    @pl.loop(0, owned, unroll=4)
    def _(slot):
        value = sums_ref[slot].astype(bf16)
        own_ref[slot] = value[:half]
        other_ref[slot] = value[half:]


def return_payload_kernel(stats, own_ref, other_ref, sums_ref, payload_ref, same_sums_ref):
    del sums_ref, same_sums_ref
    half = own_ref.shape[1]
    inside = lane_ids(half) < P_SIZE
    own = own_ref[0].astype(f32)
    other = other_ref[0].astype(f32)
    lanes = stat_lanes([read_stat(own, n) + read_stat(other, n) for n in range(stats)])

    @pl.loop(0, payload_ref.shape[0], unroll=4)
    def _(slot):
        total = own_ref[slot].astype(f32) + other_ref[slot].astype(f32)
        payload_ref[slot] = jnp.where(inside, total, lanes).astype(bf16)


def project_kernel(
    ranks, entries, own_ref, other_ref, returned_ref, basis_ref, send_ref,
    rounded_ref, payload_ref, diagonal_ref, projected_ref,
):
    owned, half, _ = own_ref.shape
    ghosts = payload_ref.shape[0]
    inside = lane_ids(half) < P_SIZE
    diagonal = read_stat(gathered_block(returned_ref, ranks), 0) / entries
    diagonal_ref[...] = jnp.broadcast_to(diagonal, (half, LANES))

    @pl.loop(0, owned, unroll=4)
    def _(face):
        projected_ref[face] = (
            own_ref[face].astype(f32)
            + other_ref[face].astype(f32)
            - diagonal * basis_ref[face, :half].astype(f32)
        )

    @pl.loop(0, ghosts)
    def _(slot):
        projected_ref[send_ref[0, slot]] += returned_ref[slot].astype(f32)

    def round_step(face, total):
        value = projected_ref[face]
        rounded_ref[face] = value.astype(bf16)
        return total + value * value

    total = slot_loop(0, owned, round_step, jnp.zeros((half, LANES), f32))
    stats = stat_lanes([masked_sum(total)]).astype(bf16)

    @pl.loop(0, ghosts, unroll=4)
    def _(slot):
        payload_ref[slot] = jnp.where(inside, rounded_ref[send_ref[0, slot]], stats)


def second_apply_kernel(
    ranks, entries, held, rounded_ref, rounded_other_ref, ghost_ref, ghost_other_ref, faces_ref, first_ref, spent_ref,
    *refs,
):
    del spent_ref
    stream = [] if held else refs[-2:]
    refs = refs if held else refs[:-2]
    *blocks_refs, basis_ref, sums_ref, ghost_own_out, ghost_other_out, norm_ref, second_ref, staging, out_sem = refs
    owned, half, _ = rounded_ref.shape
    ghosts = ghost_ref.shape[0]
    rows = 2 * half
    norm = norm_of(ghost_ref, ranks, entries)
    norm_ref[...] = jnp.broadcast_to(norm, (half, LANES))
    scale = 1.0 / norm
    scale_other = 1.0 / norm_of(ghost_other_ref, ranks, entries)

    @pl.loop(0, owned, unroll=4)
    def _(face):
        sums_ref[face] = jnp.zeros((rows, LANES), f32)
        value = (rounded_ref[face].astype(f32) * scale).astype(bf16)
        basis_ref[face, :half] = value
        staging[face] = value[:, :P_SIZE]
        basis_ref[face, half:] = (rounded_other_ref[face].astype(f32) * scale_other).astype(bf16)

    out_copy = pltpu.make_async_copy(staging, second_ref, out_sem)
    out_copy.start()
    fill_ghosts(basis_ref, sums_ref, ghost_ref, ghost_other_ref, scale, scale_other)
    field = (basis_ref, faces_ref, 2 * lax.axis_index("col"), sums_ref)
    if held:
        held_apply(blocks_refs, *field)
    else:
        streamed_apply(blocks_refs[0], *stream, *field)

    def dot_step(slot, dots):
        value = sums_ref[slot]
        return tuple(dot + basis[slot].astype(f32) * value for dot, basis in zip(dots, (first_ref, basis_ref)))

    zeros = jnp.zeros((rows, LANES), f32)
    dots = slot_loop(0, owned + ghosts, dot_step, (zeros, zeros))
    ghost_lanes(sums_ref, stat_lanes([masked_sum(dot) for dot in dots]), ghost_own_out, ghost_other_out)
    out_copy.wait()


def final_kernel(
    ranks, entries, own_ref, other_ref, returned_ref, first_ref, second_ref, send_ref, start_ref, diagonal_ref, next_ref,
    vector_ref, hessenberg_ref, image_ref,
):
    owned, half, _ = own_ref.shape
    block = gathered_block(returned_ref, ranks)
    proj_first = read_stat(block, 0) / entries
    proj_second = read_stat(block, 1) / entries

    @pl.loop(0, owned, unroll=4)
    def _(face):
        value = (
            own_ref[face].astype(f32)
            + other_ref[face].astype(f32)
            - proj_first * first_ref[face, :half].astype(f32)
        )
        image_ref[face] = value - proj_second * second_ref[face, :half].astype(f32)

    @pl.loop(0, returned_ref.shape[0])
    def _(slot):
        image_ref[send_ref[0, slot]] += returned_ref[slot].astype(f32)

    @pl.loop(0, owned, unroll=4)
    def _(face):
        vector_ref[face] = image_ref[face, :, :P_SIZE].astype(bf16)

    lanes = lane_ids(half)
    table = jnp.zeros((half, LANES), f32)
    for row, value in enumerate(
        [start_ref[...], diagonal_ref[...], next_ref[...], proj_first, proj_second]
    ):
        table = jnp.where(lanes == row, value, table)
    hessenberg_ref[...] = jnp.transpose(table)[: hessenberg_ref.shape[0]]


def call(kernel, out_shape, in_specs, scratch=(), limit=16, flops=0, bytes_accessed=0, **kwargs):
    return pl.pallas_call(
        kernel,
        out_shape=out_shape,
        in_specs=in_specs,
        scratch_shapes=scratch,
        compiler_params=pltpu.CompilerParams(vmem_limit_bytes=limit * MIB),
        cost_estimate=pl.CostEstimate(flops=flops, bytes_accessed=bytes_accessed, transcendentals=0),
        **kwargs,
    )


def body(adjoint_rhs, element_blocks, element_faces, send_faces):
    ranks = lax.axis_size("dom")
    rhs = jnp.transpose(adjoint_rhs, (0, 2, 1))
    owned, half, _ = rhs.shape
    entries = float(ranks * owned * P_SIZE)
    ghosts = send_faces.shape[1]
    elements, contracted, block_width = element_blocks.shape
    slots = owned + ghosts
    faces = element_faces.T
    raw = jnp.transpose(element_blocks, (1, 0, 2))
    group = 16
    rest = P_SIZE % group
    width = -(-block_width // LANES) * LANES
    sums_bytes = slots * 2 * half * LANES * 4
    resident = elements * 2 * LANES * width * 2 + 3 * sums_bytes <= 48 * MIB

    def out(shape, dtype=bf16):
        return pltpu.VMEM(shape, dtype) if resident else jax.ShapeDtypeStruct(shape, dtype)

    stream = [pltpu.VMEM((2, group, 2 * LANES, width), bf16), pltpu.SemaphoreType.DMA((2,))]

    def limit(amount):
        return amount if resident else 50

    def swap(value):
        return lax.ppermute(value, "col", [(0, 1), (1, 0)])

    def exchange(value):
        return lax.all_to_all(value, "dom", split_axis=0, concat_axis=0, tiled=True)

    rhs_other = swap(rhs)

    ghost_field = out((ghosts, half, LANES))
    payload = call(first_payload_kernel, ghost_field, [VMEM, SMEM], limit=limit(4))(rhs, send_faces)
    ghost = exchange(payload)

    row = jnp.arange(group * group)
    column = jnp.arange(group * group)
    perm = ((row[:, None] // group == column[None, :] % group) & (row[:, None] % group == column[None, :] // group))
    perm = perm.astype(bf16)
    tail = perm[:, : rest * group]
    raw_buffer = [pltpu.VMEM((2, contracted, group, block_width), bf16), pltpu.SemaphoreType.DMA((2,))]
    blocks_shape = (elements, 2 * LANES, width)
    parts = elements // (2 * group) if resident and elements % (2 * group) == 0 else 1
    if resident:
        operands = (raw, perm, tail)
    else:
        blocks = call(
            relayout_kernel,
            jax.ShapeDtypeStruct(blocks_shape, bf16),
            [HBM, VMEM, VMEM],
            [raw_buffer[0], stream[0], raw_buffer[1], stream[1]],
            limit=limit(20),
            out_specs=HBM,
        )(raw, perm, tail)
        operands = (blocks,)

    ghost_other = swap(ghost)

    field = out((owned, half, LANES))
    basis = out((slots, 2 * half, LANES))
    sums_field = out((slots, 2 * half, LANES), f32)
    column_values = out((half, LANES), f32)
    outs = (basis, sums_field, ghost_field, ghost_field, column_values)
    first_basis, sums, ghost_own, ghost_cross, start_norm, *blocks_held = call(
        functools.partial(first_apply_kernel, ranks, entries, resident),
        outs + ((out((elements // parts, *blocks_shape[1:])),) * parts if resident else ()),
        [VMEM] * 4 + [SMEM] + ([HBM, VMEM, VMEM] if resident else [HBM]),
        raw_buffer if resident else stream,
        limit=limit(12),
    )(rhs, rhs_other, ghost, ghost_other, faces, *operands)
    blocks = blocks_held if resident else [blocks]

    def return_payload(stats, ghost_own, ghost_cross, sums):
        return call(
            functools.partial(return_payload_kernel, stats), (ghost_field, sums_field),
            [VMEM, VMEM, ANY], limit=limit(4), input_output_aliases={2: 1}, out_specs=(VMEM, ANY),
        )(ghost_own, ghost_cross, sums)

    payload, sums = return_payload(1, ghost_own, swap(ghost_cross), sums)
    returned = exchange(payload)
    own, other = call(fields_kernel, (field, field), [VMEM], limit=limit(4))(sums)
    other = swap(other)

    rounded, payload, diagonal = call(
        functools.partial(project_kernel, ranks, entries),
        (field, ghost_field, column_values),
        [VMEM] * 4 + [SMEM],
        [pltpu.VMEM((owned, half, LANES), f32)],
        limit=limit(8),
    )(own, other, returned, first_basis, send_faces)

    rounded_other = swap(rounded)
    ghost = exchange(payload)
    ghost_other = swap(ghost)
    second_basis, sums, ghost_own, ghost_cross, next_norm, second = call(
        functools.partial(second_apply_kernel, ranks, entries, resident),
        outs + (jax.ShapeDtypeStruct((owned, half, P_SIZE), bf16),),
        [VMEM] * 4 + [SMEM, VMEM, ANY] + [VMEM if resident else HBM] * len(blocks),
        [pltpu.VMEM((owned, half, P_SIZE), bf16), pltpu.SemaphoreType.DMA] + ([] if resident else stream),
        limit=limit(6),
        out_specs=(VMEM,) * 5 + (HBM,),
        input_output_aliases={6: 1},
    )(rounded, rounded_other, ghost, ghost_other, faces, first_basis, sums, *blocks)

    payload, sums = return_payload(2, ghost_own, swap(ghost_cross), sums)
    returned = exchange(payload)
    own, other = call(fields_kernel, (field, field), [VMEM], limit=limit(4))(sums)
    other = swap(other)

    vector, hessenberg = call(
        functools.partial(final_kernel, ranks, entries),
        (jax.ShapeDtypeStruct((owned, half, P_SIZE), bf16), jax.ShapeDtypeStruct((5, half), f32)),
        [VMEM] * 5 + [SMEM] + [VMEM] * 3,
        [pltpu.VMEM((owned, half, LANES), f32)],
        limit=limit(10),
    )(own, other, returned, first_basis, second_basis, send_faces, start_norm, diagonal, next_norm)

    return (jnp.transpose(second, (0, 2, 1)), jnp.transpose(vector, (0, 2, 1)), hessenberg)


def solution(mesh):
    in_specs = (P("dom", None, "col"), P("dom", "col", None), P("dom", None), P("dom", None))
    out_specs = (P("dom", None, "col"), P("dom", None, "col"), P(None, "col"))
    return jax.shard_map(body, mesh=mesh, in_specs=in_specs, out_specs=out_specs, check_vma=False)
```

```python
import functools

import jax
import jax.numpy as jnp
from jax import lax
from jax.experimental import pallas as pl
from jax.experimental.pallas import tpu as pltpu
from jax.sharding import PartitionSpec as P

P_SIZE = 105
LANES = 128
MIB = 1 << 20
TOGETHER = 32

epsilon = 1e-06

f32 = jnp.float32
bf16 = jnp.bfloat16

VMEM = pl.BlockSpec(memory_space=pltpu.VMEM)
SMEM = pl.BlockSpec(memory_space=pltpu.SMEM)
ANY = pl.BlockSpec(memory_space=pl.ANY)
HBM = pl.BlockSpec(memory_space=pltpu.HBM)


def lane_ids(rows):
    return lax.broadcasted_iota(jnp.int32, (rows, LANES), 1)


def stat_lanes(columns):
    rows = columns[0].shape[0]
    lanes = lane_ids(rows)
    block = jnp.zeros((rows, LANES), f32)
    lane = P_SIZE
    for value in columns:
        rest = value * 0.5
        for _ in range(3):
            part = rest.astype(bf16).astype(f32)
            block = jnp.where(lanes == lane, part, block)
            rest = rest - part
            lane += 1
    return block


def read_stat(block, which):
    lanes = lane_ids(block.shape[0])
    first = P_SIZE + 3 * which
    inside = (lanes >= first) & (lanes < first + 3)
    return 2.0 * jnp.sum(jnp.where(inside, block, 0.0), axis=1, keepdims=True)


def gathered_block(ghost_ref, ranks):
    slots = ghost_ref.shape[0] // ranks
    total = ghost_ref[0].astype(f32)
    for rank in range(1, ranks):
        total = total + ghost_ref[rank * slots].astype(f32)
    return total


def first_payload_kernel(rhs_ref, send_ref, payload_ref, held, sems, listed, listed_sem):
    faces, rows, _ = rhs_ref.shape
    parts = sems.shape[0]
    count = faces // parts

    def copy(part):
        span = pl.ds(part * count, count)
        return pltpu.make_async_copy(rhs_ref.at[span], held.at[span], sems.at[part])

    for part in range(parts):
        copy(part).start()
    list_copy = pltpu.make_async_copy(send_ref, listed, listed_sem)
    list_copy.start()

    def add(face, total):
        value = held[face].astype(f32)
        return total + value * value

    total = jnp.zeros((rows, P_SIZE), f32)
    for part in range(parts):
        copy(part).wait()
        total = lax.fori_loop(part * count, (part + 1) * count, add, total, unroll=8)
    stats = stat_lanes([jnp.sum(total, axis=1, keepdims=True)]).astype(bf16)
    list_copy.wait()

    @pl.loop(0, payload_ref.shape[0], unroll=4)
    def _(slot):
        payload_ref[slot] = stats
        payload_ref[slot, :, :P_SIZE] = held[listed[0, slot]]


def relayout(source, perm_ref, tail_ref, target):
    group = source.shape[1]
    width = source.shape[2]
    full = P_SIZE // group
    rest = P_SIZE - full * group
    for slot in range(source.shape[0] // P_SIZE):
        for part in range(full + 1):
            first = slot * P_SIZE + part * group
            depth = group if part < full else rest
            chunk = source[first : first + depth].reshape(depth * group, width)
            perm = perm_ref[...] if part < full else tail_ref[...]
            moved = jnp.dot(perm, chunk, preferred_element_type=f32).astype(bf16)
            for element in range(group):
                target[element, pl.ds(slot * LANES + part * group, group), :width] = moved[
                    element * group : (element + 1) * group
                ]
        zeros = jnp.zeros((LANES - (full + 1) * group, target.shape[2]), bf16)
        for element in range(group):
            target[element, pl.ds(slot * LANES + (full + 1) * group, zeros.shape[0]), :] = zeros


def copy_group(source_ref, buffer, sems, step):
    group = buffer.shape[2]
    return pltpu.make_async_copy(
        source_ref.at[:, pl.ds(step * group, group), :], buffer.at[step % 2], sems.at[step % 2]
    )


def relayout_kernel(raw_ref, perm_ref, tail_ref, out_ref, buffer, staging, sems, out_sems):
    group = buffer.shape[2]
    steps = raw_ref.shape[1] // group

    def copy_out(step):
        return pltpu.make_async_copy(
            staging.at[step % 2], out_ref.at[pl.ds(step * group, group)], out_sems.at[step % 2]
        )

    copy_group(raw_ref, buffer, sems, 0).start()
    for step in range(steps):
        if step + 1 < steps:
            copy_group(raw_ref, buffer, sems, step + 1).start()
        copy_group(raw_ref, buffer, sems, step).wait()
        if step >= 2:
            copy_out(step - 2).wait()
        relayout(buffer.at[step % 2], perm_ref, tail_ref, staging.at[step % 2])
        copy_out(step).start()
    for step in range(max(0, steps - 2), steps):
        copy_out(step).wait()


def slot_pieces(terms):
    lanes = lane_ids(terms.shape[0])
    tiles = [terms[:, LANES * n : LANES * (n + 1)] for n in range(4)]
    pieces = [tiles[0]]
    for slot in range(1, 4):
        shift = slot * (LANES - P_SIZE)
        pieces.append(
            jnp.where(lanes < shift, pltpu.roll(tiles[slot - 1], shift, 1), pltpu.roll(tiles[slot], shift, 1))
        )
    return pieces


def add_terms(first, blocks, basis_ref, faces_ref, first_slot, sums_ref):
    pieces = []
    for inner, block in enumerate(blocks):
        left = basis_ref[faces_ref[first_slot, first + inner]]
        right = basis_ref[faces_ref[first_slot + 1, first + inner]]
        terms = jnp.dot(jnp.concatenate([left, right], axis=1), block(), preferred_element_type=f32)
        for slot, piece in enumerate(slot_pieces(terms)):
            pieces.append((faces_ref[slot, first + inner], piece))
    for slot, piece in pieces:
        sums_ref[slot] += piece


def held_apply(blocks_refs, *refs):
    first = 0
    for blocks_ref in blocks_refs:
        count = blocks_ref.shape[0]
        together = max(n for n in range(1, TOGETHER + 1) if count % n == 0)

        @pl.loop(0, count // together)
        def _(step, blocks_ref=blocks_ref, first=first, together=together):
            at = step * together
            add_terms(first + at, [lambda n=n: blocks_ref[at + n] for n in range(together)], *refs)

        first += count


def streamed_apply(blocks_ref, buffer, sems, *refs):
    group = buffer.shape[1]
    steps = blocks_ref.shape[0] // group

    def copy(step):
        return pltpu.make_async_copy(
            blocks_ref.at[pl.ds(step * group, group)], buffer.at[step % 2], sems.at[step % 2]
        )

    copy(0).start()
    for step in range(steps):
        if step + 1 < steps:
            copy(step + 1).start()
        copy(step).wait()
        add_terms(step * group, [lambda n=n: buffer[step % 2, n] for n in range(group)], *refs)


def relayout_apply(raw_ref, perm_ref, tail_ref, blocks_refs, buffer, sems, *refs):
    group = buffer.shape[2]
    targets = [
        (blocks_ref, first) for blocks_ref in blocks_refs for first in range(0, blocks_ref.shape[0], group)
    ]
    def apply_step(step):
        target, first = targets[step]
        add_terms(step * group, [lambda n=n: target[first + n] for n in range(group)], *refs)

    for step, (target, first) in enumerate(targets):
        copy_group(raw_ref, buffer, sems, step).wait()
        relayout(buffer.at[step % 2], perm_ref, tail_ref, target.at[pl.ds(first, group)])
        if step:
            apply_step(step - 1)
        if step + 2 < len(targets):
            copy_group(raw_ref, buffer, sems, step + 2).start()
    apply_step(len(targets) - 1)


def masked_sum(value):
    return jnp.sum(jnp.where(lane_ids(value.shape[0]) < P_SIZE, value, 0.0), axis=1, keepdims=True)


def slot_loop(first, last, step, carry):
    return lax.fori_loop(first, last, step, carry, unroll=4)


def ghost_lanes(sums_ref, stats, ghost_own_out, ghost_other_out):
    ghosts, half, _ = ghost_own_out.shape
    owned = sums_ref.shape[0] - ghosts
    inside = lane_ids(2 * half) < P_SIZE

    @pl.loop(0, ghosts, unroll=4)
    def _(slot):
        value = jnp.where(inside, sums_ref[owned + slot], stats).astype(bf16)
        ghost_own_out[slot] = value[:half]
        ghost_other_out[slot] = value[half:]


def norm_of(ghost_ref, ranks, entries):
    return jnp.sqrt(read_stat(gathered_block(ghost_ref, ranks), 0) / entries + epsilon)


def fill_ghosts(basis_ref, sums_ref, ghost_ref, ghost_other_ref, scale, scale_other):
    ghosts, half, _ = ghost_ref.shape
    owned = sums_ref.shape[0] - ghosts
    inside = lane_ids(half) < P_SIZE

    @pl.loop(0, ghosts, unroll=4)
    def _(slot):
        sums_ref[owned + slot] = jnp.zeros((2 * half, LANES), f32)
        basis_ref[owned + slot, :half] = jnp.where(inside, ghost_ref[slot].astype(f32) * scale, 0.0).astype(bf16)
        basis_ref[owned + slot, half:] = jnp.where(
            inside, ghost_other_ref[slot].astype(f32) * scale_other, 0.0
        ).astype(bf16)


def first_apply_kernel(
    ranks, entries, fused, rhs_ref, rhs_other_ref, ghost_ref, ghost_other_ref, faces_ref, *refs,
):
    owned, half, _ = rhs_ref.shape
    ghosts = ghost_ref.shape[0]
    rows = 2 * half
    if fused:
        raw_ref, perm_ref, tail_ref, *outs, buffer, sems = refs
        blocks_refs = outs[5:]
        for step in range(2):
            copy_group(raw_ref, buffer, sems, step).start()
    else:
        blocks_ref, *outs, buffer, sems = refs
    basis_ref, sums_ref, ghost_own_out, ghost_other_out, norm_ref = outs[:5]

    norm = norm_of(ghost_ref, ranks, entries)
    norm_ref[...] = jnp.broadcast_to(norm, (half, LANES))
    scale = 1.0 / norm
    scale_other = 1.0 / norm_of(ghost_other_ref, ranks, entries)

    @pl.loop(0, owned, unroll=4)
    def _(face):
        sums_ref[face] = jnp.zeros((rows, LANES), f32)
        basis_ref[face] = jnp.zeros((rows, LANES), bf16)
        basis_ref[face, :half, :P_SIZE] = (rhs_ref[face].astype(f32) * scale).astype(bf16)
        basis_ref[face, half:, :P_SIZE] = (rhs_other_ref[face].astype(f32) * scale_other).astype(bf16)

    fill_ghosts(basis_ref, sums_ref, ghost_ref, ghost_other_ref, scale, scale_other)
    field = (basis_ref, faces_ref, 2 * lax.axis_index("col"), sums_ref)
    if fused:
        relayout_apply(raw_ref, perm_ref, tail_ref, blocks_refs, buffer, sems, *field)
    else:
        streamed_apply(blocks_ref, buffer, sems, *field)

    def dot_step(slot, dot):
        return dot + basis_ref[slot].astype(f32) * sums_ref[slot]

    dot = slot_loop(0, owned + ghosts, dot_step, jnp.zeros((rows, LANES), f32))
    ghost_lanes(sums_ref, stat_lanes([masked_sum(dot)]), ghost_own_out, ghost_other_out)


def fields_kernel(sums_ref, own_ref, other_ref):
    owned, half, _ = own_ref.shape

    @pl.loop(0, owned, unroll=4)
    def _(slot):
        value = sums_ref[slot].astype(bf16)
        own_ref[slot] = value[:half]
        other_ref[slot] = value[half:]


def return_payload_kernel(stats, own_ref, other_ref, sums_ref, payload_ref, same_sums_ref):
    del sums_ref, same_sums_ref
    half = own_ref.shape[1]
    inside = lane_ids(half) < P_SIZE
    own = own_ref[0].astype(f32)
    other = other_ref[0].astype(f32)
    lanes = stat_lanes([read_stat(own, n) + read_stat(other, n) for n in range(stats)])

    @pl.loop(0, payload_ref.shape[0], unroll=4)
    def _(slot):
        total = own_ref[slot].astype(f32) + other_ref[slot].astype(f32)
        payload_ref[slot] = jnp.where(inside, total, lanes).astype(bf16)


def project_kernel(
    ranks, entries, own_ref, other_ref, returned_ref, basis_ref, send_ref,
    rounded_ref, payload_ref, diagonal_ref, projected_ref,
):
    owned, half, _ = own_ref.shape
    ghosts = payload_ref.shape[0]
    inside = lane_ids(half) < P_SIZE
    diagonal = read_stat(gathered_block(returned_ref, ranks), 0) / entries
    diagonal_ref[...] = jnp.broadcast_to(diagonal, (half, LANES))

    @pl.loop(0, owned, unroll=4)
    def _(face):
        projected_ref[face] = (
            own_ref[face].astype(f32)
            + other_ref[face].astype(f32)
            - diagonal * basis_ref[face, :half].astype(f32)
        )

    @pl.loop(0, ghosts)
    def _(slot):
        projected_ref[send_ref[0, slot]] += returned_ref[slot].astype(f32)

    def round_step(face, total):
        value = projected_ref[face]
        rounded_ref[face] = value.astype(bf16)
        return total + value * value

    total = slot_loop(0, owned, round_step, jnp.zeros((half, LANES), f32))
    stats = stat_lanes([masked_sum(total)]).astype(bf16)

    @pl.loop(0, ghosts, unroll=4)
    def _(slot):
        payload_ref[slot] = jnp.where(inside, rounded_ref[send_ref[0, slot]], stats)


def second_apply_kernel(
    ranks, entries, held, rounded_ref, rounded_other_ref, ghost_ref, ghost_other_ref, faces_ref, first_ref, spent_ref,
    *refs,
):
    del spent_ref
    stream = [] if held else refs[-2:]
    refs = refs if held else refs[:-2]
    *blocks_refs, basis_ref, sums_ref, ghost_own_out, ghost_other_out, norm_ref, second_ref, staging, out_sem = refs
    owned, half, _ = rounded_ref.shape
    ghosts = ghost_ref.shape[0]
    rows = 2 * half
    norm = norm_of(ghost_ref, ranks, entries)
    norm_ref[...] = jnp.broadcast_to(norm, (half, LANES))
    scale = 1.0 / norm
    scale_other = 1.0 / norm_of(ghost_other_ref, ranks, entries)

    @pl.loop(0, owned, unroll=4)
    def _(face):
        sums_ref[face] = jnp.zeros((rows, LANES), f32)
        value = (rounded_ref[face].astype(f32) * scale).astype(bf16)
        basis_ref[face, :half] = value
        staging[face] = value[:, :P_SIZE]
        basis_ref[face, half:] = (rounded_other_ref[face].astype(f32) * scale_other).astype(bf16)

    out_copy = pltpu.make_async_copy(staging, second_ref, out_sem)
    out_copy.start()
    fill_ghosts(basis_ref, sums_ref, ghost_ref, ghost_other_ref, scale, scale_other)
    field = (basis_ref, faces_ref, 2 * lax.axis_index("col"), sums_ref)
    if held:
        held_apply(blocks_refs, *field)
    else:
        streamed_apply(blocks_refs[0], *stream, *field)

    def dot_step(slot, dots):
        value = sums_ref[slot]
        return tuple(dot + basis[slot].astype(f32) * value for dot, basis in zip(dots, (first_ref, basis_ref)))

    zeros = jnp.zeros((rows, LANES), f32)
    dots = slot_loop(0, owned + ghosts, dot_step, (zeros, zeros))
    ghost_lanes(sums_ref, stat_lanes([masked_sum(dot) for dot in dots]), ghost_own_out, ghost_other_out)
    out_copy.wait()


def final_kernel(
    ranks, entries, own_ref, other_ref, returned_ref, first_ref, second_ref, send_ref, start_ref, diagonal_ref, next_ref,
    vector_ref, hessenberg_ref, image_ref,
):
    owned, half, _ = own_ref.shape
    block = gathered_block(returned_ref, ranks)
    proj_first = read_stat(block, 0) / entries
    proj_second = read_stat(block, 1) / entries

    @pl.loop(0, owned, unroll=4)
    def _(face):
        value = (
            own_ref[face].astype(f32)
            + other_ref[face].astype(f32)
            - proj_first * first_ref[face, :half].astype(f32)
        )
        image_ref[face] = value - proj_second * second_ref[face, :half].astype(f32)

    @pl.loop(0, returned_ref.shape[0])
    def _(slot):
        image_ref[send_ref[0, slot]] += returned_ref[slot].astype(f32)

    @pl.loop(0, owned, unroll=4)
    def _(face):
        vector_ref[face] = image_ref[face, :, :P_SIZE].astype(bf16)

    lanes = lane_ids(half)
    table = jnp.zeros((half, LANES), f32)
    for row, value in enumerate(
        [start_ref[...], diagonal_ref[...], next_ref[...], proj_first, proj_second]
    ):
        table = jnp.where(lanes == row, value, table)
    hessenberg_ref[...] = jnp.transpose(table)[: hessenberg_ref.shape[0]]


def call(kernel, out_shape, in_specs, scratch=(), limit=16, flops=0, bytes_accessed=0, **kwargs):
    return pl.pallas_call(
        kernel,
        out_shape=out_shape,
        in_specs=in_specs,
        scratch_shapes=scratch,
        compiler_params=pltpu.CompilerParams(vmem_limit_bytes=limit * MIB),
        cost_estimate=pl.CostEstimate(flops=flops, bytes_accessed=bytes_accessed, transcendentals=0),
        **kwargs,
    )


def body(adjoint_rhs, element_blocks, element_faces, send_faces):
    ranks = lax.axis_size("dom")
    rhs = jnp.transpose(adjoint_rhs, (0, 2, 1))
    owned, half, _ = rhs.shape
    entries = float(ranks * owned * P_SIZE)
    ghosts = send_faces.shape[1]
    elements, contracted, block_width = element_blocks.shape
    slots = owned + ghosts
    faces = element_faces.T
    raw = jnp.transpose(element_blocks, (1, 0, 2))
    group = 16
    rest = P_SIZE % group
    width = -(-block_width // LANES) * LANES
    sums_bytes = slots * 2 * half * LANES * 4
    resident = elements * 2 * LANES * width * 2 + 3 * sums_bytes <= 48 * MIB

    def out(shape, dtype=bf16):
        return pltpu.VMEM(shape, dtype) if resident else jax.ShapeDtypeStruct(shape, dtype)

    stream = [pltpu.VMEM((2, group, 2 * LANES, width), bf16), pltpu.SemaphoreType.DMA((2,))]

    def limit(amount):
        return amount if resident else 50

    def swap(value):
        return lax.ppermute(value, "col", [(0, 1), (1, 0)])

    def exchange(value):
        return lax.all_to_all(value, "dom", split_axis=0, concat_axis=0, tiled=True)

    rhs_other = swap(rhs)

    ghost_field = out((ghosts, half, LANES))
    arriving = 4 if owned % 4 == 0 else 1
    payload = call(
        first_payload_kernel, ghost_field, [HBM, HBM],
        [
            pltpu.VMEM((owned, half, P_SIZE), bf16), pltpu.SemaphoreType.DMA((arriving,)),
            pltpu.SMEM(send_faces.shape, jnp.int32), pltpu.SemaphoreType.DMA,
        ],
        limit=limit(4),
    )(pltpu.with_memory_space_constraint(rhs, pltpu.HBM), pltpu.with_memory_space_constraint(send_faces, pltpu.HBM))
    ghost = exchange(payload)

    row = jnp.arange(group * group)
    column = jnp.arange(group * group)
    perm = ((row[:, None] // group == column[None, :] % group) & (row[:, None] % group == column[None, :] // group))
    perm = perm.astype(bf16)
    tail = perm[:, : rest * group]
    raw_buffer = [pltpu.VMEM((2, contracted, group, block_width), bf16), pltpu.SemaphoreType.DMA((2,))]
    blocks_shape = (elements, 2 * LANES, width)
    parts = elements // (2 * group) if resident and elements % (2 * group) == 0 else 1
    if resident:
        operands = (raw, perm, tail)
    else:
        blocks = call(
            relayout_kernel,
            jax.ShapeDtypeStruct(blocks_shape, bf16),
            [HBM, VMEM, VMEM],
            [raw_buffer[0], stream[0], raw_buffer[1], stream[1]],
            limit=limit(20),
            out_specs=HBM,
        )(raw, perm, tail)
        operands = (blocks,)

    ghost_other = swap(ghost)

    field = out((owned, half, LANES))
    basis = out((slots, 2 * half, LANES))
    sums_field = out((slots, 2 * half, LANES), f32)
    column_values = out((half, LANES), f32)
    outs = (basis, sums_field, ghost_field, ghost_field, column_values)
    first_basis, sums, ghost_own, ghost_cross, start_norm, *blocks_held = call(
        functools.partial(first_apply_kernel, ranks, entries, resident),
        outs + ((out((elements // parts, *blocks_shape[1:])),) * parts if resident else ()),
        [VMEM] * 4 + [SMEM] + ([HBM, VMEM, VMEM] if resident else [HBM]),
        raw_buffer if resident else stream,
        limit=limit(12),
    )(rhs, rhs_other, ghost, ghost_other, faces, *operands)
    blocks = blocks_held if resident else [blocks]

    def return_payload(stats, ghost_own, ghost_cross, sums):
        return call(
            functools.partial(return_payload_kernel, stats), (ghost_field, sums_field),
            [VMEM, VMEM, ANY], limit=limit(4), input_output_aliases={2: 1}, out_specs=(VMEM, ANY),
        )(ghost_own, ghost_cross, sums)

    payload, sums = return_payload(1, ghost_own, swap(ghost_cross), sums)
    returned = exchange(payload)
    own, other = call(fields_kernel, (field, field), [VMEM], limit=limit(4))(sums)
    other = swap(other)

    rounded, payload, diagonal = call(
        functools.partial(project_kernel, ranks, entries),
        (field, ghost_field, column_values),
        [VMEM] * 4 + [SMEM],
        [pltpu.VMEM((owned, half, LANES), f32)],
        limit=limit(8),
    )(own, other, returned, first_basis, send_faces)

    rounded_other = swap(rounded)
    ghost = exchange(payload)
    ghost_other = swap(ghost)
    second_basis, sums, ghost_own, ghost_cross, next_norm, second = call(
        functools.partial(second_apply_kernel, ranks, entries, resident),
        outs + (jax.ShapeDtypeStruct((owned, half, P_SIZE), bf16),),
        [VMEM] * 4 + [SMEM, VMEM, ANY] + [VMEM if resident else HBM] * len(blocks),
        [pltpu.VMEM((owned, half, P_SIZE), bf16), pltpu.SemaphoreType.DMA] + ([] if resident else stream),
        limit=limit(6),
        out_specs=(VMEM,) * 5 + (HBM,),
        input_output_aliases={6: 1},
    )(rounded, rounded_other, ghost, ghost_other, faces, first_basis, sums, *blocks)

    payload, sums = return_payload(2, ghost_own, swap(ghost_cross), sums)
    returned = exchange(payload)
    own, other = call(fields_kernel, (field, field), [VMEM], limit=limit(4))(sums)
    other = swap(other)

    vector, hessenberg = call(
        functools.partial(final_kernel, ranks, entries),
        (jax.ShapeDtypeStruct((owned, half, P_SIZE), bf16), jax.ShapeDtypeStruct((5, half), f32)),
        [VMEM] * 5 + [SMEM] + [VMEM] * 3,
        [pltpu.VMEM((owned, half, LANES), f32)],
        limit=limit(10),
    )(own, other, returned, first_basis, second_basis, send_faces, start_norm, diagonal, next_norm)

    return (jnp.transpose(second, (0, 2, 1)), jnp.transpose(vector, (0, 2, 1)), hessenberg)


def solution(mesh):
    in_specs = (P("dom", None, "col"), P("dom", "col", None), P("dom", None), P("dom", None))
    out_specs = (P("dom", None, "col"), P("dom", None, "col"), P(None, "col"))
    return jax.shard_map(body, mesh=mesh, in_specs=in_specs, out_specs=out_specs, check_vma=False)
```

```python
import functools

import jax
import jax.numpy as jnp
from jax import lax
from jax.experimental import pallas as pl
from jax.experimental.pallas import tpu as pltpu
from jax.sharding import PartitionSpec as P

P_SIZE = 105
LANES = 128
MIB = 1 << 20
TOGETHER = 32

epsilon = 1e-06

f32 = jnp.float32
bf16 = jnp.bfloat16

VMEM = pl.BlockSpec(memory_space=pltpu.VMEM)
SMEM = pl.BlockSpec(memory_space=pltpu.SMEM)
ANY = pl.BlockSpec(memory_space=pl.ANY)
HBM = pl.BlockSpec(memory_space=pltpu.HBM)


def lane_ids(rows):
    return lax.broadcasted_iota(jnp.int32, (rows, LANES), 1)


def stat_lanes(columns):
    rows = columns[0].shape[0]
    lanes = lane_ids(rows)
    block = jnp.zeros((rows, LANES), f32)
    lane = P_SIZE
    for value in columns:
        rest = value * 0.5
        for _ in range(3):
            part = rest.astype(bf16).astype(f32)
            block = jnp.where(lanes == lane, part, block)
            rest = rest - part
            lane += 1
    return block


def read_stat(block, which):
    lanes = lane_ids(block.shape[0])
    first = P_SIZE + 3 * which
    inside = (lanes >= first) & (lanes < first + 3)
    return 2.0 * jnp.sum(jnp.where(inside, block, 0.0), axis=1, keepdims=True)


def gathered_block(ghost_ref, ranks):
    slots = ghost_ref.shape[0] // ranks
    total = ghost_ref[0].astype(f32)
    for rank in range(1, ranks):
        total = total + ghost_ref[rank * slots].astype(f32)
    return total


def first_payload_kernel(rhs_ref, send_ref, payload_ref, held, sems, listed, listed_sem):
    faces, rows, _ = rhs_ref.shape
    parts = sems.shape[0]
    count = faces // parts

    def copy(part):
        span = pl.ds(part * count, count)
        return pltpu.make_async_copy(rhs_ref.at[span], held.at[span], sems.at[part])

    for part in range(parts):
        copy(part).start()
    list_copy = pltpu.make_async_copy(send_ref, listed, listed_sem)
    list_copy.start()

    def add(face, total):
        value = held[face].astype(f32)
        return total + value * value

    total = jnp.zeros((rows, P_SIZE), f32)
    for part in range(parts):
        copy(part).wait()
        total = lax.fori_loop(part * count, (part + 1) * count, add, total, unroll=8)
    stats = stat_lanes([jnp.sum(total, axis=1, keepdims=True)]).astype(bf16)
    list_copy.wait()

    @pl.loop(0, payload_ref.shape[0], unroll=4)
    def _(slot):
        payload_ref[slot] = stats
        payload_ref[slot, :, :P_SIZE] = held[listed[0, slot]]


def relayout(source, perm_ref, tail_ref, target):
    group = source.shape[1]
    width = source.shape[2]
    full = P_SIZE // group
    rest = P_SIZE - full * group
    for slot in range(source.shape[0] // P_SIZE):
        for part in range(full + 1):
            first = slot * P_SIZE + part * group
            depth = group if part < full else rest
            chunk = source[first : first + depth].reshape(depth * group, width)
            perm = perm_ref[...] if part < full else tail_ref[...]
            moved = jnp.dot(perm, chunk, preferred_element_type=f32).astype(bf16)
            for element in range(group):
                target[element, pl.ds(slot * LANES + part * group, group), :width] = moved[
                    element * group : (element + 1) * group
                ]
        zeros = jnp.zeros((LANES - (full + 1) * group, target.shape[2]), bf16)
        for element in range(group):
            target[element, pl.ds(slot * LANES + (full + 1) * group, zeros.shape[0]), :] = zeros


def copy_group(source_ref, buffer, sems, step):
    group = buffer.shape[2]
    return pltpu.make_async_copy(
        source_ref.at[:, pl.ds(step * group, group), :], buffer.at[step % 2], sems.at[step % 2]
    )


def relayout_kernel(raw_ref, perm_ref, tail_ref, out_ref, buffer, staging, sems, out_sems):
    group = buffer.shape[2]
    steps = raw_ref.shape[1] // group

    def copy_out(step):
        return pltpu.make_async_copy(
            staging.at[step % 2], out_ref.at[pl.ds(step * group, group)], out_sems.at[step % 2]
        )

    copy_group(raw_ref, buffer, sems, 0).start()
    for step in range(steps):
        if step + 1 < steps:
            copy_group(raw_ref, buffer, sems, step + 1).start()
        copy_group(raw_ref, buffer, sems, step).wait()
        if step >= 2:
            copy_out(step - 2).wait()
        relayout(buffer.at[step % 2], perm_ref, tail_ref, staging.at[step % 2])
        copy_out(step).start()
    for step in range(max(0, steps - 2), steps):
        copy_out(step).wait()


def slot_pieces(terms):
    lanes = lane_ids(terms.shape[0])
    tiles = [terms[:, LANES * n : LANES * (n + 1)] for n in range(4)]
    pieces = [tiles[0]]
    for slot in range(1, 4):
        shift = slot * (LANES - P_SIZE)
        pieces.append(
            jnp.where(lanes < shift, pltpu.roll(tiles[slot - 1], shift, 1), pltpu.roll(tiles[slot], shift, 1))
        )
    return pieces


def add_terms(first, blocks, basis_ref, faces_ref, first_slot, sums_ref):
    pieces = []
    for inner, block in enumerate(blocks):
        left = basis_ref[faces_ref[first_slot, first + inner]]
        right = basis_ref[faces_ref[first_slot + 1, first + inner]]
        terms = jnp.dot(jnp.concatenate([left, right], axis=1), block(), preferred_element_type=f32)
        for slot, piece in enumerate(slot_pieces(terms)):
            pieces.append((faces_ref[slot, first + inner], piece))
    for slot, piece in pieces:
        sums_ref[slot] += piece


def held_apply(blocks_refs, *refs):
    first = 0
    for blocks_ref in blocks_refs:
        count = blocks_ref.shape[0]
        together = max(n for n in range(1, TOGETHER + 1) if count % n == 0)

        @pl.loop(0, count // together)
        def _(step, blocks_ref=blocks_ref, first=first, together=together):
            at = step * together
            add_terms(first + at, [lambda n=n: blocks_ref[at + n] for n in range(together)], *refs)

        first += count


def streamed_apply(blocks_ref, buffer, sems, *refs):
    group = buffer.shape[1]
    steps = blocks_ref.shape[0] // group

    def copy(step):
        return pltpu.make_async_copy(
            blocks_ref.at[pl.ds(step * group, group)], buffer.at[step % 2], sems.at[step % 2]
        )

    copy(0).start()
    for step in range(steps):
        if step + 1 < steps:
            copy(step + 1).start()
        copy(step).wait()
        add_terms(step * group, [lambda n=n: buffer[step % 2, n] for n in range(group)], *refs)


def relayout_apply(raw_ref, perm_ref, tail_ref, blocks_refs, buffer, sems, *refs):
    group = buffer.shape[2]
    targets = [
        (blocks_ref, first) for blocks_ref in blocks_refs for first in range(0, blocks_ref.shape[0], group)
    ]
    def apply_step(step):
        target, first = targets[step]
        add_terms(step * group, [lambda n=n: target[first + n] for n in range(group)], *refs)

    for step, (target, first) in enumerate(targets):
        copy_group(raw_ref, buffer, sems, step).wait()
        relayout(buffer.at[step % 2], perm_ref, tail_ref, target.at[pl.ds(first, group)])
        if step:
            apply_step(step - 1)
        if step + 2 < len(targets):
            copy_group(raw_ref, buffer, sems, step + 2).start()
    apply_step(len(targets) - 1)


def masked_sum(value):
    return jnp.sum(jnp.where(lane_ids(value.shape[0]) < P_SIZE, value, 0.0), axis=1, keepdims=True)


def slot_loop(first, last, step, carry):
    return lax.fori_loop(first, last, step, carry, unroll=4)


def ghost_lanes(sums_ref, stats, ghost_own_out, ghost_other_out):
    ghosts, half, _ = ghost_own_out.shape
    owned = sums_ref.shape[0] - ghosts
    inside = lane_ids(2 * half) < P_SIZE

    @pl.loop(0, ghosts, unroll=4)
    def _(slot):
        value = jnp.where(inside, sums_ref[owned + slot], stats).astype(bf16)
        ghost_own_out[slot] = value[:half]
        ghost_other_out[slot] = value[half:]


def norm_of(ghost_ref, ranks, entries):
    return jnp.sqrt(read_stat(gathered_block(ghost_ref, ranks), 0) / entries + epsilon)


def fill_ghosts(basis_ref, sums_ref, ghost_ref, ghost_other_ref, scale, scale_other):
    ghosts, half, _ = ghost_ref.shape
    owned = sums_ref.shape[0] - ghosts
    inside = lane_ids(half) < P_SIZE

    @pl.loop(0, ghosts, unroll=4)
    def _(slot):
        sums_ref[owned + slot] = jnp.zeros((2 * half, LANES), f32)
        basis_ref[owned + slot, :half] = jnp.where(inside, ghost_ref[slot].astype(f32) * scale, 0.0).astype(bf16)
        basis_ref[owned + slot, half:] = jnp.where(
            inside, ghost_other_ref[slot].astype(f32) * scale_other, 0.0
        ).astype(bf16)


def first_apply_kernel(
    ranks, entries, fused, rhs_ref, rhs_other_ref, ghost_ref, ghost_other_ref, faces_ref, *refs,
):
    owned, half, _ = rhs_ref.shape
    ghosts = ghost_ref.shape[0]
    rows = 2 * half
    if fused:
        raw_ref, perm_ref, tail_ref, *outs, buffer, sems = refs
        blocks_refs = outs[5:]
        for step in range(2):
            copy_group(raw_ref, buffer, sems, step).start()
    else:
        blocks_ref, *outs, buffer, sems = refs
    basis_ref, sums_ref, ghost_own_out, ghost_other_out, norm_ref = outs[:5]

    norm = norm_of(ghost_ref, ranks, entries)
    norm_ref[...] = jnp.broadcast_to(norm, (half, LANES))
    scale = 1.0 / norm
    scale_other = 1.0 / norm_of(ghost_other_ref, ranks, entries)

    @pl.loop(0, owned, unroll=4)
    def _(face):
        sums_ref[face] = jnp.zeros((rows, LANES), f32)
        spare = jnp.zeros((half, LANES - P_SIZE), f32)
        own = jnp.concatenate([rhs_ref[face].astype(f32) * scale, spare], axis=1)
        other = jnp.concatenate([rhs_other_ref[face].astype(f32) * scale_other, spare], axis=1)
        basis_ref[face, :half] = own.astype(bf16)
        basis_ref[face, half:] = other.astype(bf16)

    fill_ghosts(basis_ref, sums_ref, ghost_ref, ghost_other_ref, scale, scale_other)
    field = (basis_ref, faces_ref, 2 * lax.axis_index("col"), sums_ref)
    if fused:
        relayout_apply(raw_ref, perm_ref, tail_ref, blocks_refs, buffer, sems, *field)
    else:
        streamed_apply(blocks_ref, buffer, sems, *field)

    def dot_step(slot, dot):
        return dot + basis_ref[slot].astype(f32) * sums_ref[slot]

    dot = slot_loop(0, owned + ghosts, dot_step, jnp.zeros((rows, LANES), f32))
    ghost_lanes(sums_ref, stat_lanes([masked_sum(dot)]), ghost_own_out, ghost_other_out)


def fields_kernel(sums_ref, own_ref, other_ref):
    owned, half, _ = own_ref.shape

    @pl.loop(0, owned, unroll=4)
    def _(slot):
        value = sums_ref[slot].astype(bf16)
        own_ref[slot] = value[:half]
        other_ref[slot] = value[half:]


def return_payload_kernel(stats, own_ref, other_ref, sums_ref, payload_ref, same_sums_ref):
    del sums_ref, same_sums_ref
    half = own_ref.shape[1]
    inside = lane_ids(half) < P_SIZE
    own = own_ref[0].astype(f32)
    other = other_ref[0].astype(f32)
    lanes = stat_lanes([read_stat(own, n) + read_stat(other, n) for n in range(stats)])

    @pl.loop(0, payload_ref.shape[0], unroll=4)
    def _(slot):
        total = own_ref[slot].astype(f32) + other_ref[slot].astype(f32)
        payload_ref[slot] = jnp.where(inside, total, lanes).astype(bf16)


def project_kernel(
    ranks, entries, own_ref, other_ref, returned_ref, basis_ref, send_ref,
    rounded_ref, payload_ref, diagonal_ref, projected_ref,
):
    owned, half, _ = own_ref.shape
    ghosts = payload_ref.shape[0]
    inside = lane_ids(half) < P_SIZE
    diagonal = read_stat(gathered_block(returned_ref, ranks), 0) / entries
    diagonal_ref[...] = jnp.broadcast_to(diagonal, (half, LANES))

    @pl.loop(0, owned, unroll=4)
    def _(face):
        projected_ref[face] = (
            own_ref[face].astype(f32)
            + other_ref[face].astype(f32)
            - diagonal * basis_ref[face, :half].astype(f32)
        )

    @pl.loop(0, ghosts, unroll=8)
    def _(slot):
        projected_ref[send_ref[0, slot]] += returned_ref[slot].astype(f32)

    def round_step(face, total):
        value = projected_ref[face]
        rounded_ref[face] = value.astype(bf16)
        return total + value * value

    total = slot_loop(0, owned, round_step, jnp.zeros((half, LANES), f32))
    stats = stat_lanes([masked_sum(total)]).astype(bf16)

    @pl.loop(0, ghosts, unroll=4)
    def _(slot):
        payload_ref[slot] = jnp.where(inside, rounded_ref[send_ref[0, slot]], stats)


def second_apply_kernel(
    ranks, entries, held, rounded_ref, rounded_other_ref, ghost_ref, ghost_other_ref, faces_ref, first_ref, spent_ref,
    *refs,
):
    del spent_ref
    stream = [] if held else refs[-2:]
    refs = refs if held else refs[:-2]
    *blocks_refs, basis_ref, sums_ref, ghost_own_out, ghost_other_out, norm_ref, second_ref, staging, out_sem = refs
    owned, half, _ = rounded_ref.shape
    ghosts = ghost_ref.shape[0]
    rows = 2 * half
    norm = norm_of(ghost_ref, ranks, entries)
    norm_ref[...] = jnp.broadcast_to(norm, (half, LANES))
    scale = 1.0 / norm
    scale_other = 1.0 / norm_of(ghost_other_ref, ranks, entries)

    @pl.loop(0, owned, unroll=4)
    def _(face):
        sums_ref[face] = jnp.zeros((rows, LANES), f32)
        value = (rounded_ref[face].astype(f32) * scale).astype(bf16)
        basis_ref[face, :half] = value
        staging[face] = value[:, :P_SIZE]
        basis_ref[face, half:] = (rounded_other_ref[face].astype(f32) * scale_other).astype(bf16)

    out_copy = pltpu.make_async_copy(staging, second_ref, out_sem)
    out_copy.start()
    fill_ghosts(basis_ref, sums_ref, ghost_ref, ghost_other_ref, scale, scale_other)
    field = (basis_ref, faces_ref, 2 * lax.axis_index("col"), sums_ref)
    if held:
        held_apply(blocks_refs, *field)
    else:
        streamed_apply(blocks_refs[0], *stream, *field)

    def dot_step(slot, dots):
        value = sums_ref[slot]
        return tuple(dot + basis[slot].astype(f32) * value for dot, basis in zip(dots, (first_ref, basis_ref)))

    zeros = jnp.zeros((rows, LANES), f32)
    dots = slot_loop(0, owned + ghosts, dot_step, (zeros, zeros))
    ghost_lanes(sums_ref, stat_lanes([masked_sum(dot) for dot in dots]), ghost_own_out, ghost_other_out)
    out_copy.wait()


def final_kernel(
    ranks, entries, own_ref, other_ref, returned_ref, first_ref, second_ref, send_ref, start_ref, diagonal_ref, next_ref,
    vector_ref, hessenberg_ref, image_ref,
):
    owned, half, _ = own_ref.shape
    block = gathered_block(returned_ref, ranks)
    proj_first = read_stat(block, 0) / entries
    proj_second = read_stat(block, 1) / entries

    @pl.loop(0, owned, unroll=4)
    def _(face):
        value = (
            own_ref[face].astype(f32)
            + other_ref[face].astype(f32)
            - proj_first * first_ref[face, :half].astype(f32)
        )
        image_ref[face] = value - proj_second * second_ref[face, :half].astype(f32)

    @pl.loop(0, returned_ref.shape[0], unroll=8)
    def _(slot):
        image_ref[send_ref[0, slot]] += returned_ref[slot].astype(f32)

    @pl.loop(0, owned, unroll=4)
    def _(face):
        vector_ref[face] = image_ref[face, :, :P_SIZE].astype(bf16)

    lanes = lane_ids(half)
    table = jnp.zeros((half, LANES), f32)
    for row, value in enumerate(
        [start_ref[...], diagonal_ref[...], next_ref[...], proj_first, proj_second]
    ):
        table = jnp.where(lanes == row, value, table)
    hessenberg_ref[...] = jnp.transpose(table)[: hessenberg_ref.shape[0]]


def call(kernel, out_shape, in_specs, scratch=(), limit=16, flops=0, bytes_accessed=0, **kwargs):
    return pl.pallas_call(
        kernel,
        out_shape=out_shape,
        in_specs=in_specs,
        scratch_shapes=scratch,
        compiler_params=pltpu.CompilerParams(vmem_limit_bytes=limit * MIB),
        cost_estimate=pl.CostEstimate(flops=flops, bytes_accessed=bytes_accessed, transcendentals=0),
        **kwargs,
    )


def body(adjoint_rhs, element_blocks, element_faces, send_faces):
    ranks = lax.axis_size("dom")
    rhs = jnp.transpose(adjoint_rhs, (0, 2, 1))
    owned, half, _ = rhs.shape
    entries = float(ranks * owned * P_SIZE)
    ghosts = send_faces.shape[1]
    elements, contracted, block_width = element_blocks.shape
    slots = owned + ghosts
    faces = element_faces.T
    raw = jnp.transpose(element_blocks, (1, 0, 2))
    group = 16
    rest = P_SIZE % group
    width = -(-block_width // LANES) * LANES
    sums_bytes = slots * 2 * half * LANES * 4
    resident = elements * 2 * LANES * width * 2 + 3 * sums_bytes <= 48 * MIB

    def out(shape, dtype=bf16):
        return pltpu.VMEM(shape, dtype) if resident else jax.ShapeDtypeStruct(shape, dtype)

    stream = [pltpu.VMEM((2, group, 2 * LANES, width), bf16), pltpu.SemaphoreType.DMA((2,))]

    def limit(amount):
        return amount if resident else 50

    def swap(value):
        return lax.ppermute(value, "col", [(0, 1), (1, 0)])

    def exchange(value):
        return lax.all_to_all(value, "dom", split_axis=0, concat_axis=0, tiled=True)

    rhs_other = swap(rhs)

    ghost_field = out((ghosts, half, LANES))
    arriving = 4 if owned % 4 == 0 else 1
    payload = call(
        first_payload_kernel, ghost_field, [HBM, HBM],
        [
            pltpu.VMEM((owned, half, P_SIZE), bf16), pltpu.SemaphoreType.DMA((arriving,)),
            pltpu.SMEM(send_faces.shape, jnp.int32), pltpu.SemaphoreType.DMA,
        ],
        limit=limit(4),
    )(pltpu.with_memory_space_constraint(rhs, pltpu.HBM), pltpu.with_memory_space_constraint(send_faces, pltpu.HBM))
    ghost = exchange(payload)

    row = jnp.arange(group * group)
    column = jnp.arange(group * group)
    perm = ((row[:, None] // group == column[None, :] % group) & (row[:, None] % group == column[None, :] // group))
    perm = perm.astype(bf16)
    tail = perm[:, : rest * group]
    raw_buffer = [pltpu.VMEM((2, contracted, group, block_width), bf16), pltpu.SemaphoreType.DMA((2,))]
    blocks_shape = (elements, 2 * LANES, width)
    parts = elements // (2 * group) if resident and elements % (2 * group) == 0 else 1
    if resident:
        operands = (raw, perm, tail)
    else:
        blocks = call(
            relayout_kernel,
            jax.ShapeDtypeStruct(blocks_shape, bf16),
            [HBM, VMEM, VMEM],
            [raw_buffer[0], stream[0], raw_buffer[1], stream[1]],
            limit=limit(20),
            out_specs=HBM,
        )(raw, perm, tail)
        operands = (blocks,)

    ghost_other = swap(ghost)

    field = out((owned, half, LANES))
    basis = out((slots, 2 * half, LANES))
    sums_field = out((slots, 2 * half, LANES), f32)
    column_values = out((half, LANES), f32)
    outs = (basis, sums_field, ghost_field, ghost_field, column_values)
    first_basis, sums, ghost_own, ghost_cross, start_norm, *blocks_held = call(
        functools.partial(first_apply_kernel, ranks, entries, resident),
        outs + ((out((elements // parts, *blocks_shape[1:])),) * parts if resident else ()),
        [VMEM] * 4 + [SMEM] + ([HBM, VMEM, VMEM] if resident else [HBM]),
        raw_buffer if resident else stream,
        limit=limit(12),
    )(rhs, rhs_other, ghost, ghost_other, faces, *operands)
    blocks = blocks_held if resident else [blocks]

    def return_payload(stats, ghost_own, ghost_cross, sums):
        return call(
            functools.partial(return_payload_kernel, stats), (ghost_field, sums_field),
            [VMEM, VMEM, ANY], limit=limit(4), input_output_aliases={2: 1}, out_specs=(VMEM, ANY),
        )(ghost_own, ghost_cross, sums)

    payload, sums = return_payload(1, ghost_own, swap(ghost_cross), sums)
    returned = exchange(payload)
    own, other = call(fields_kernel, (field, field), [VMEM], limit=limit(4))(sums)
    other = swap(other)

    rounded, payload, diagonal = call(
        functools.partial(project_kernel, ranks, entries),
        (field, ghost_field, column_values),
        [VMEM] * 4 + [SMEM],
        [pltpu.VMEM((owned, half, LANES), f32)],
        limit=limit(8),
    )(own, other, returned, first_basis, send_faces)

    rounded_other = swap(rounded)
    ghost = exchange(payload)
    ghost_other = swap(ghost)
    second_basis, sums, ghost_own, ghost_cross, next_norm, second = call(
        functools.partial(second_apply_kernel, ranks, entries, resident),
        outs + (jax.ShapeDtypeStruct((owned, half, P_SIZE), bf16),),
        [VMEM] * 4 + [SMEM, VMEM, ANY] + [VMEM if resident else HBM] * len(blocks),
        [pltpu.VMEM((owned, half, P_SIZE), bf16), pltpu.SemaphoreType.DMA] + ([] if resident else stream),
        limit=limit(6),
        out_specs=(VMEM,) * 5 + (HBM,),
        input_output_aliases={6: 1},
    )(rounded, rounded_other, ghost, ghost_other, faces, first_basis, sums, *blocks)

    payload, sums = return_payload(2, ghost_own, swap(ghost_cross), sums)
    returned = exchange(payload)
    own, other = call(fields_kernel, (field, field), [VMEM], limit=limit(4))(sums)
    other = swap(other)

    vector, hessenberg = call(
        functools.partial(final_kernel, ranks, entries),
        (jax.ShapeDtypeStruct((owned, half, P_SIZE), bf16), jax.ShapeDtypeStruct((5, half), f32)),
        [VMEM] * 5 + [SMEM] + [VMEM] * 3,
        [pltpu.VMEM((owned, half, LANES), f32)],
        limit=limit(10),
    )(own, other, returned, first_basis, second_basis, send_faces, start_norm, diagonal, next_norm)

    return (jnp.transpose(second, (0, 2, 1)), jnp.transpose(vector, (0, 2, 1)), hessenberg)


def solution(mesh):
    in_specs = (P("dom", None, "col"), P("dom", "col", None), P("dom", None), P("dom", None))
    out_specs = (P("dom", None, "col"), P("dom", None, "col"), P(None, "col"))
    return jax.shard_map(body, mesh=mesh, in_specs=in_specs, out_specs=out_specs, check_vma=False)
```
